32 devices in a mesh: shot: 2 (over y), gx: 4 (over z), sec: 2 (over x), gy: 2 (over core).
Axes of the slice: x: 2, y: 2, z: 4, core: 2. Of those that a mesh axis runs over, the one named last changes fastest.
Arguments:
- source_fields: float32 [8, 16, 32, 256], P('shot', 'sec', 'gx', 'gy'), parts along dimension 0, may hold values from -6 to 6
- receiver_fields: float32 [8, 16, 32, 256], P('shot', 'sec', 'gx', 'gy'), parts along dimension 0, may hold values from -6 to 6
- courant: float32 [16, 32, 256], P('sec', 'gx', 'gy'), may hold values from 0.05 to 0.15
- epsilon: float32 [16, 32, 256], P('sec', 'gx', 'gy'), may hold values from 0.05 to 0.3
- delta_param: float32 [16, 32, 256], P('sec', 'gx', 'gy'), may hold values from 0 to 0.15
- tilt_angle: float32 [16, 32, 256], P('sec', 'gx', 'gy'), may hold values from -0.8 to 0.8
- source_pos: int32 [6], P('shot'), parts along dimension 0, may hold values from 0 to 255, as said below
- wavelet: float32 [18], P('shot'), parts along dimension 0, may hold values from -24 to 24
- receiver_pos: int32 [512, 3], P('shot'), parts along dimension 0, may hold values from 0 to 255, as said below
- receiver_data: float32 [18, 256], P('shot'), parts along dimension 0, may hold values from -6 to 6
- step_counts: int32 [3], replicated, may hold values from 1 to 3, as said below
- offset_lags: int32 [48, 2], replicated, may hold values from -8 to 8, as said below
Outputs:
- offset_images: bfloat16 [96, 16, 32, 256], P('shot', 'sec', 'gx', 'gy'), parts along dimension 0
- source_out: float32 [8, 16, 32, 256], P('shot', 'sec', 'gx', 'gy'), parts along dimension 0
- receiver_out: float32 [8, 16, 32, 256], P('shot', 'sec', 'gx', 'gy'), parts along dimension 0
The draws below stay inside these ranges and needn't reach their ends.
There are 2 independent parts, one for each index of `shot`. The reference program is written for one: setup_inputs(seed, part) draws one part's arguments, and reference() takes and returns one part's arrays. A program takes and returns all parts, laid end to end along the dimension named above; an argument that names none is the same for every part. Nothing has to cross between parts.
Inputs may be any that keep to these rules, and one draw needn't show every extreme that they name: `source_pos`: a grid cell: depth below 16, first horizontal below 32, second horizontal below 256; it lies on the last cell of the longest grid dimension and on cell 0 of another dimension. `receiver_pos`: grid cells: depth below 16, first horizontal below 32, second horizontal below 256; one receiver sits at the far corner of the grid and one at its anchor. `step_counts`: some snapshot takes all 3 steps. `offset_lags`: in each dimension some lag is 8 and some is minus 8.
All inputs are finite; a program needn't handle non-finite values.
Results may differ from the reference program's by a relative error of at most 0.001.
The reference program's roundings to bfloat16 on the way count: a program that leaves them out, or rounds other values in their place, can miss the bound.
Values may be sent and summed in bfloat16 or wider, within the bound.
A program may use at most 64 MiB of HBM per device.

```python
import math
import jax
import jax.numpy as jnp
from jax import lax

SNAPS = 3
STEPS = 3
NLAG = 48
LAG = 8
NREC = 256
NZ = 16
NX = 32
NY = 256
TSLOTS = 9


def draw_cells(key, count):
    keys = jax.random.split(key, 3)
    depth_idx = jax.random.randint(keys[0], (count,), 0, NZ)
    first_idx = jax.random.randint(keys[1], (count,), 0, NX)
    second_idx = jax.random.randint(keys[2], (count,), 0, NY)
    return jnp.stack([depth_idx, first_idx, second_idx], axis=1).astype(jnp.int32)


def draw_source_pos(key, part):
    cell = draw_cells(jax.random.fold_in(key, 11), 1).reshape(3)
    bounds = [NZ, NX, NY]
    longest = 0
    for position in range(3):
        if bounds[position] > bounds[longest]:
            longest = position
    other = (longest + 1) % 3
    slots = lax.iota(jnp.int32, 3)
    cell = jnp.where(slots == longest, bounds[longest] - 1, cell)
    cell = jnp.where(slots == other, 0, cell)
    return cell.astype(jnp.int32)


def draw_receiver_pos(key, part):
    cells = draw_cells(jax.random.fold_in(key, 23), NREC)
    rows = lax.iota(jnp.int32, NREC)[:, None]
    corner = jnp.array([[NZ - 1, NX - 1, NY - 1]], jnp.int32)
    cells = jnp.where(rows == 0, corner, cells)
    cells = jnp.where(rows == 1, 0, cells)
    return cells.astype(jnp.int32)


def draw_step_counts(key, part):
    keys = jax.random.split(jax.random.fold_in(key, 37), 2)
    counts = jax.random.randint(keys[0], (SNAPS,), 1, STEPS + 1)
    chosen = jax.random.randint(keys[1], (), 0, SNAPS)
    return jnp.where(lax.iota(jnp.int32, SNAPS) == chosen, STEPS, counts).astype(jnp.int32)


def draw_offset_lags(key, part):
    keys = jax.random.split(jax.random.fold_in(key, 41), 3)
    values = jax.random.randint(keys[0], (NLAG, 2), -LAG, LAG + 1)
    first_row = jax.random.randint(keys[1], (), 0, NLAG)
    second_row = (first_row + 1 + jax.random.randint(keys[2], (), 0, NLAG - 1)) % NLAG
    rows = lax.iota(jnp.int32, NLAG)[:, None]
    values = jnp.where(rows == first_row, jnp.array([[LAG, -LAG]], jnp.int32), values)
    values = jnp.where(rows == second_row, jnp.array([[-LAG, LAG]], jnp.int32), values)
    return values.astype(jnp.int32)


def block_scale(rng, extent, cuts, smallest, high):
    loudness = 1.0
    for dim, shards_of in cuts:
        steps = jax.random.uniform(jax.random.fold_in(jax.random.fold_in(rng, 6), dim), (shards_of,), jnp.float32, smallest / len(cuts), high / len(cuts))
        loudness = loudness * jnp.repeat(jnp.exp(steps), extent[dim] // shards_of).reshape((-1,) + (1,) * (len(extent) - 1 - dim))
    return loudness


def normal_values(key, shape, deviation, limit, shards=(), kind=jnp.bfloat16):
    drawn = deviation * jax.random.normal(key, shape, jnp.float32)
    if shards:
        drawn = drawn * block_scale(key, shape, shards, -0.22, 0.18)
    return jnp.clip(drawn, -limit, limit).astype(kind)


def setup_inputs(seed: int = 0, part: int = 0) -> dict:
    arg_keys = jax.random.split(jax.random.key(seed), 13)
    part_keys = jax.random.split(jax.random.fold_in(arg_keys[12], part), 13)
    source_fields = normal_values(part_keys[0], (4, NZ, NX, NY), 1.0, 6.0, ((1, 2), (2, 4), (3, 2)), jnp.float32)
    receiver_fields = normal_values(part_keys[1], (4, NZ, NX, NY), 1.0, 6.0, ((1, 2), (2, 4), (3, 2)), jnp.float32)
    courant = jnp.clip(jnp.exp(math.log(0.15) - 1.0986123 * jax.random.uniform(arg_keys[2], (NZ, NX, NY), jnp.float32) ** block_scale(arg_keys[2], (NZ, NX, NY), ((0, 2), (1, 4), (2, 2)), -0.2, 0.2)), 0.05, 0.15)
    epsilon = jnp.clip(0.05 + 0.25 * jax.random.uniform(arg_keys[3], (NZ, NX, NY), jnp.float32) ** block_scale(arg_keys[3], (NZ, NX, NY), ((0, 2), (1, 4), (2, 2)), -0.2, 0.2), 0.05, 0.3)
    delta_param = jnp.clip(0.15 * jax.random.uniform(arg_keys[4], (NZ, NX, NY), jnp.float32) ** block_scale(arg_keys[4], (NZ, NX, NY), ((0, 2), (1, 4), (2, 2)), -0.2, 0.2), 0.0, 0.15)
    tilt_angle = jnp.clip(jax.random.uniform(arg_keys[5], (NZ, NX, NY), jnp.float32, -0.8, 0.8) * block_scale(arg_keys[5], (NZ, NX, NY), ((0, 2), (1, 4), (2, 2)), -0.4, 0.0), -0.8, 0.8)
    source_pos = draw_source_pos(jax.random.fold_in(jax.random.fold_in(arg_keys[12], part), 71), part)
    wavelet = normal_values(part_keys[7], (TSLOTS,), 6.0, 24.0, (), jnp.float32)
    receiver_pos = draw_receiver_pos(jax.random.fold_in(jax.random.fold_in(arg_keys[12], part), 71), part)
    receiver_data = normal_values(part_keys[9], (TSLOTS, NREC), 1.0, 6.0, (), jnp.float32)
    step_counts = draw_step_counts(jax.random.fold_in(arg_keys[12], 71), part)
    offset_lags = draw_offset_lags(jax.random.fold_in(arg_keys[12], 71), part)
    return dict(source_fields=source_fields, receiver_fields=receiver_fields, courant=courant, epsilon=epsilon, delta_param=delta_param, tilt_angle=tilt_angle, source_pos=source_pos, wavelet=wavelet, receiver_pos=receiver_pos, receiver_data=receiver_data, step_counts=step_counts, offset_lags=offset_lags)


def coefficients(courant, epsilon, delta_param, tilt_angle):
    cos_tilt = jnp.cos(tilt_angle)
    sin_tilt = jnp.sin(tilt_angle)
    return (courant, 1.0 + 2.0 * epsilon, 1.0 + 2.0 * delta_param, cos_tilt * cos_tilt, sin_tilt * sin_tilt, 2.0 * sin_tilt * cos_tilt)


def second_diffs(padded):
    center = padded[..., 1:-1, 1:-1, 1:-1]
    along_z = padded[..., 2:, 1:-1, 1:-1] + padded[..., :-2, 1:-1, 1:-1] - 2.0 * center
    along_x = padded[..., 1:-1, 2:, 1:-1] + padded[..., 1:-1, :-2, 1:-1] - 2.0 * center
    along_y = padded[..., 1:-1, 1:-1, 2:] + padded[..., 1:-1, 1:-1, :-2] - 2.0 * center
    cross_xz = 0.25 * (padded[..., 2:, 2:, 1:-1] - padded[..., 2:, :-2, 1:-1] - padded[..., :-2, 2:, 1:-1] + padded[..., :-2, :-2, 1:-1])
    return along_z, along_x, along_y, cross_xz


def advance(padded_p, padded_q, pressure, auxiliary, pressure_old, auxiliary_old, coeffs):
    courant, gain_eps, gain_delta, weight_z, weight_x, weight_mixed = coeffs
    p_zz, p_xx, p_yy, p_xz = second_diffs(padded_p)
    vert_p = weight_z * p_zz + weight_x * p_xx + weight_mixed * p_xz
    horiz_p = p_zz + p_xx + p_yy - vert_p
    q_zz, q_xx, _, q_xz = second_diffs(padded_q)
    vert_q = weight_z * q_zz + weight_x * q_xx + weight_mixed * q_xz
    new_p = 2.0 * pressure - pressure_old + courant * (gain_eps * horiz_p + vert_q)
    new_q = 2.0 * auxiliary - auxiliary_old + courant * (gain_delta * horiz_p + vert_q)
    return new_p, new_q


def deposit(field_3d, points, amounts):
    return field_3d.at[points[:, 0], points[:, 1], points[:, 2]].add(amounts)


def reference(source_fields, receiver_fields, courant, epsilon, delta_param, tilt_angle, source_pos, wavelet, receiver_pos, receiver_data, step_counts, offset_lags):
    coeffs = coefficients(courant, epsilon, delta_param, tilt_angle)
    sections = [[source_fields[member] for member in range(4)], [receiver_fields[member] for member in range(4)]]
    positions = [source_pos.reshape(1, 3), receiver_pos]
    snapshots = []
    for snapshot in range(SNAPS):
        for substep in range(STEPS):
            time_slot = snapshot * STEPS + substep
            active = substep < step_counts[snapshot]
            amounts = [wavelet[time_slot].reshape(1), receiver_data[time_slot]]
            for section in range(2):
                pressure, auxiliary, pressure_old, auxiliary_old = sections[section]
                new_p, new_q = advance(jnp.pad(pressure, 1), jnp.pad(auxiliary, 1), pressure, auxiliary, pressure_old, auxiliary_old, coeffs)
                new_p = deposit(new_p, positions[section], amounts[section])
                new_q = deposit(new_q, positions[section], amounts[section])
                sections[section] = [jnp.where(active, new_p, pressure), jnp.where(active, new_q, auxiliary), jnp.where(active, pressure, pressure_old), jnp.where(active, auxiliary, auxiliary_old)]
        widen = ((0, 0), (LAG, LAG), (LAG, LAG))
        snapshots.append((jnp.pad(sections[0][0].astype(jnp.bfloat16), widen), jnp.pad(sections[1][0].astype(jnp.bfloat16), widen)))

    def image_lag(lag_pair):
        shift_x = lag_pair[0].astype(jnp.int32)
        shift_y = lag_pair[1].astype(jnp.int32)
        start_zero = jnp.zeros((), jnp.int32)
        summed = jnp.zeros((NZ, NX, NY), jnp.float32)
        for source_snap, receiver_snap in snapshots:
            source_win = lax.dynamic_slice(source_snap, (start_zero, (LAG - shift_x).astype(jnp.int32), (LAG - shift_y).astype(jnp.int32)), (NZ, NX, NY))
            receiver_win = lax.dynamic_slice(receiver_snap, (start_zero, (LAG + shift_x).astype(jnp.int32), (LAG + shift_y).astype(jnp.int32)), (NZ, NX, NY))
            summed = summed + source_win.astype(jnp.float32) * receiver_win.astype(jnp.float32)
        return summed

    images = lax.map(image_lag, offset_lags).astype(jnp.bfloat16)
    return images, jnp.stack(sections[0]), jnp.stack(sections[1])
```

```python
import functools

import jax
import jax.numpy as jnp
from jax import lax
from jax.experimental import pallas as pl
from jax.experimental.pallas import tpu as pltpu
from jax.sharding import PartitionSpec as P

SNAPS = 3
STEPS = 3
LAG = 8

MESH = pl.DeviceIdType.MESH

HALO_X = ((-1, 0), (1, 0))
HALO_Z = ((0, -1), (0, 1))
HALO_XZ = ((-1, -1), (-1, 1), (1, -1), (1, 1))


def kernel(
    sizes,
    src_ref,
    rec_ref,
    cou_ref,
    eps_ref,
    del_ref,
    tilt_ref,
    spos_ref,
    wav_ref,
    rpos_ref,
    rdat_ref,
    cnt_ref,
    lag_ref,
    img_ref,
    so_ref,
    ro_ref,
    ext,
    old,
    yhalo,
    xsend,
    xrecv,
    dsend,
    drecv,
    coef,
    dep,
    shot,
    snap_send,
    snap_recv,
    centre,
    beside,
    acc,
    halo_ssem,
    halo_rsem,
    snap_ssem,
    snap_rsem,
):
    nz, nx, ny = cou_ref.shape
    nlag = lag_ref.shape[0]
    lo, hi = nx, 2 * nx
    ngx, nsec, ngy = sizes
    gx, sec, gy = lax.axis_index("gx"), lax.axis_index("sec"), lax.axis_index("gy")
    ypart = 1 - gy

    def inside(dx, dz):
        ok = None
        if dx:
            ok = gx > 0 if dx < 0 else gx < ngx - 1
        if dz:
            okz = sec > 0 if dz < 0 else sec < nsec - 1
            ok = okz if ok is None else jnp.logical_and(ok, okz)
        return ok

    def device(dx, dz, other):
        where = {}
        if dx:
            where["gx"] = gx + dx
        if dz:
            where["sec"] = sec + dz
        if other:
            where["gy"] = ypart
        return where

    ext[...] = jnp.zeros_like(ext)
    ext[0, 0, 1 : 1 + nz, lo:hi, :] = src_ref[0]
    ext[0, 2, 1 : 1 + nz, lo:hi, :] = src_ref[1]
    ext[0, 1, 1 : 1 + nz, lo:hi, :] = rec_ref[0]
    ext[0, 3, 1 : 1 + nz, lo:hi, :] = rec_ref[1]
    old[0] = src_ref[2]
    old[2] = src_ref[3]
    old[1] = rec_ref[2]
    old[3] = rec_ref[3]

    barrier = pltpu.get_barrier_semaphore()
    greeted = [(dx, dz, False) for dx, dz in HALO_X + HALO_Z + HALO_XZ]
    greeted += [(-1, 0, True), (1, 0, True)]
    total = jnp.int32(1)
    pl.semaphore_signal(barrier, inc=1, device_id=device(0, 0, True), device_id_type=MESH)
    for dx, dz, other in greeted:
        ok = inside(dx, dz)
        total = total + ok.astype(jnp.int32)

        @pl.when(ok)
        def _():
            pl.semaphore_signal(
                barrier, inc=1, device_id=device(dx, dz, other), device_id_type=MESH
            )

    lane = lax.broadcasted_iota(jnp.int32, (nx, ny), 1)
    keep = (lane < ny // 2) == (gy == 0)
    first_lane = lane == 0
    last_lane = lane == ny - 1

    def copies(par):
        made = []
        n = 0

        def add(ok, src, dst, where):
            nonlocal n
            made.append(
                (
                    ok,
                    pltpu.make_async_remote_copy(
                        src_ref=src,
                        dst_ref=dst,
                        send_sem=halo_ssem.at[par, n],
                        recv_sem=halo_rsem.at[par, n],
                        device_id=where,
                        device_id_type=MESH,
                    ),
                )
            )
            n += 1

        for i, (dx, dz) in enumerate(HALO_X):
            add(inside(dx, dz), xsend.at[par, i], xrecv.at[par, i], device(dx, dz, False))
        for dx, dz in HALO_Z:
            here, there = (1, 1 + nz) if dz < 0 else (nz, 0)
            add(
                inside(dx, dz),
                ext.at[par, :, here, lo:hi, :],
                ext.at[par, :, there, lo:hi, :],
                device(dx, dz, False),
            )
        for i, (dx, dz) in enumerate(HALO_XZ):
            add(inside(dx, dz), dsend.at[par, i], drecv.at[par, i], device(dx, dz, False))
        add(
            None,
            ext.at[par, 0:2, 1 : 1 + nz, lo:hi, :],
            yhalo.at[par],
            device(0, 0, True),
        )
        return made

    ways = list(HALO_X + HALO_Z + HALO_XZ)

    def guarded(ok, action):
        if ok is None:
            action()
        else:
            pl.when(ok)(action)

    def send_halos(par):
        for f in range(4):
            for i, (dx, _) in enumerate(HALO_X):
                row = lo if dx < 0 else hi - 1
                for z in range(nz):
                    xsend[par, i, f, z : z + 1, :] = ext[par, f, 1 + z, row : row + 1, :]
            for i, (dx, dz) in enumerate(HALO_XZ):
                row = lo if dx < 0 else hi - 1
                plane = 1 if dz < 0 else nz
                dsend[par, i, f : f + 1, :] = ext[par, f, plane, row : row + 1, :]
        for ok, copy in copies(par):
            guarded(ok, copy.start)

    def wait_halos(par):
        made = copies(par)
        for n, (dx, dz) in enumerate(ways):
            guarded(inside(-dx, -dz), made[n][1].wait_recv)
        made[-1][1].wait_recv()
        for i, (dx, dz) in enumerate(HALO_X):
            row = hi if dx < 0 else lo - 1

            def place():
                for f in range(4):
                    for z in range(nz):
                        ext[par, f, 1 + z, row : row + 1, :] = xrecv[par, i, f, z : z + 1, :]

            pl.when(inside(-dx, -dz))(place)
        for i, (dx, dz) in enumerate(HALO_XZ):
            row = hi if dx < 0 else lo - 1
            plane = 1 + nz if dz < 0 else 0

            def place():
                for f in range(4):
                    ext[par, f, plane, row : row + 1, :] = drecv[par, i, f : f + 1, :]

            pl.when(inside(-dx, -dz))(place)

    def wait_sends(par):
        for ok, copy in copies(par):
            guarded(ok, copy.wait_send)

    def snap_copies(s):
        made = []
        for n, (dx, other) in enumerate(
            ((-1, False), (1, False), (0, True), (-1, True), (1, True))
        ):
            made.append(
                (
                    dx,
                    other,
                    pltpu.make_async_remote_copy(
                        src_ref=snap_send.at[s],
                        dst_ref=snap_recv.at[s, n],
                        send_sem=snap_ssem.at[s, n],
                        recv_sem=snap_rsem.at[s, n],
                        device_id=device(dx, 0, other),
                        device_id_type=MESH,
                    ),
                )
            )
        return made

    def take_snapshot(s, par):
        for h in range(2):
            rounded = ext[par, h, 1 : 1 + nz, lo:hi, :].astype(jnp.bfloat16)
            snap_send[s, h] = rounded.reshape(nz * nx, ny)
            centre[h, :, lo:hi, :] = rounded.astype(jnp.float32)

    def send_snapshot(s):
        for dx, other, copy in snap_copies(s):
            guarded(inside(dx, 0) if dx else None, copy.start)

    def wait_snapshot(s):
        for n, (dx, other, copy) in enumerate(snap_copies(s)):

            def place():
                copy.wait_recv()
                first = lo - dx * nx
                target = beside if other else centre
                for h in range(2):
                    block = snap_recv[s, n, h].astype(jnp.float32).reshape(nz, nx, ny)
                    if other:
                        block = jnp.where(keep[None], block, 0.0)
                    target[h, :, first : first + nx, :] = block

            guarded(inside(-dx, 0) if dx else None, place)

    def wait_snapshot_sends(s):
        for dx, other, copy in snap_copies(s):
            guarded(inside(dx, 0) if dx else None, copy.wait_send)

    def image(s, first, last):
        def one_lag(lag, carry):
            lx = lag_ref[lag, 0]
            ly = lag_ref[lag, 1]

            def window(h, sx, sy):
                c = centre[h, :, pl.ds(lo + sx, nx), :]
                b = beside[h, :, pl.ds(lo + sx, nx), :]
                edge = jnp.logical_or(lane < sy, lane >= ny + sy)
                mixed = jnp.where(edge[None], b, c)
                return pltpu.roll(mixed, lax.rem(ny - sy, ny), 2)

            product = window(0, -lx, -ly) * window(1, lx, ly)
            product = product.reshape(nz * nx, ny)
            if s == 0:
                acc[lag] = product
            elif s < SNAPS - 1:
                acc[lag] = acc[lag] + product
            else:
                img_ref[lag] = (acc[lag] + product).astype(jnp.bfloat16)
            return carry

        lax.fori_loop(first, last, one_lag, 0)

    def prepare():
        tilt = tilt_ref[...]
        cos_tilt, sin_tilt = jnp.cos(tilt), jnp.sin(tilt)
        coef[0] = cou_ref[...]
        coef[1] = 1.0 + 2.0 * eps_ref[...]
        coef[2] = 1.0 + 2.0 * del_ref[...]
        coef[3] = cos_tilt * cos_tilt
        coef[4] = sin_tilt * sin_tilt
        coef[5] = 2.0 * sin_tilt * cos_tilt
        zi = lax.broadcasted_iota(jnp.int32, (nz, nx, ny), 0) + sec * nz
        xi = lax.broadcasted_iota(jnp.int32, (nz, nx, ny), 1) + gx * nx
        yi = lax.broadcasted_iota(jnp.int32, (nz, nx, ny), 2) + gy * ny
        hit = (zi == spos_ref[0]) & (xi == spos_ref[1]) & (yi == spos_ref[2])
        shot[...] = jnp.where(hit, 1.0, 0.0)
        nrec = rpos_ref.shape[1]
        rz = rpos_ref[0:1, :] - sec * nz
        rx = rpos_ref[1:2, :] - gx * nx
        ry = rpos_ref[2:3, :] - gy * ny
        okx = (rx >= 0) & (rx < nx)
        cell = jnp.where(okx, rz * nx + rx, -1)
        at_cell = lax.broadcasted_iota(jnp.int32, (nz * nx, nrec), 0) == cell
        at_y = lax.broadcasted_iota(jnp.int32, (ny, nrec), 0) == ry
        at_y = jnp.where(at_y, 1.0, 0.0).astype(jnp.bfloat16)
        for t in range(SNAPS * STEPS):
            left = rdat_ref[t : t + 1, :]
            summed = jnp.zeros((nz * nx, ny), jnp.float32)
            for _ in range(3):
                part = left.astype(jnp.bfloat16).astype(jnp.float32)
                left = left - part
                rows = jnp.where(at_cell, part, 0.0).astype(jnp.bfloat16)
                summed = summed + lax.dot_general(
                    rows, at_y, (((1,), (1,)), ((), ())), preferred_element_type=jnp.float32
                )
            dep[t] = summed.reshape(nz, nx, ny)

    def compute(k, par, active):
        nxt = 1 - par
        for z in range(nz):
            cou, ge, gd = coef[0, z], coef[1, z], coef[2, z]
            wz, wx, wm = coef[3, z], coef[4, z], coef[5, z]

            def diffs(f):
                def at(dz, dx):
                    return ext[par, f, 1 + z + dz, lo + dx : hi + dx, :]

                c = at(0, 0)
                zz = at(1, 0) + at(-1, 0) - 2.0 * c
                xx = at(0, 1) + at(0, -1) - 2.0 * c
                xz = 0.25 * (at(1, 1) - at(1, -1) - at(-1, 1) + at(-1, -1))
                return c, zz, xx, xz

            for h in range(2):
                p, pzz, pxx, pxz = diffs(h)
                q, qzz, qxx, qxz = diffs(2 + h)
                w = jnp.where(keep, yhalo[par, h, z], 0.0)
                above = pltpu.roll(jnp.where(first_lane, w, p), ny - 1, 1)
                below = pltpu.roll(jnp.where(last_lane, w, p), 1, 1)
                pyy = above + below - 2.0 * p
                vert_p = wz * pzz + wx * pxx + wm * pxz
                horiz = pzz + pxx + pyy - vert_p
                vert_q = wz * qzz + wx * qxx + wm * qxz
                p_old, q_old = old[h, z], old[2 + h, z]
                amount = shot[z] * wav_ref[k] if h == 0 else dep[k, z]
                new_p = 2.0 * p - p_old + cou * (ge * horiz + vert_q) + amount
                new_q = 2.0 * q - q_old + cou * (gd * horiz + vert_q) + amount
                ext[nxt, h, 1 + z, lo:hi, :] = jnp.where(active, new_p, p)
                ext[nxt, 2 + h, 1 + z, lo:hi, :] = jnp.where(active, new_q, q)
                old[h, z] = jnp.where(active, p, p_old)
                old[2 + h, z] = jnp.where(active, q, q_old)

    centre[...] = jnp.zeros_like(centre)
    beside[...] = jnp.zeros_like(beside)
    pl.semaphore_wait(barrier, total)

    chunk = -(-nlag // STEPS)
    for s in range(SNAPS):

        def step(j, carry):
            k = s * STEPS + j
            par = lax.rem(k, 2)
            send_halos(par)
            if s == 0:
                pl.when(j == 0)(prepare)
            else:

                @pl.when(j == 0)
                def _():
                    send_snapshot(s - 1)

                @pl.when(j == 1)
                def _():
                    wait_snapshot(s - 1)
                    image(s - 1, 0, nlag // 2)

                @pl.when(j == 2)
                def _():
                    image(s - 1, nlag // 2, nlag)

            wait_halos(par)
            compute(k, par, j < cnt_ref[s])
            wait_sends(par)
            return carry

        lax.fori_loop(0, STEPS, step, 0)
        take_snapshot(s, (s * STEPS + STEPS) % 2)

    last = SNAPS - 1
    send_snapshot(last)
    par = (SNAPS * STEPS) % 2
    for h, out in enumerate((so_ref, ro_ref)):
        out[0] = ext[par, h, 1 : 1 + nz, lo:hi, :]
        out[1] = ext[par, 2 + h, 1 : 1 + nz, lo:hi, :]
        out[2] = old[h]
        out[3] = old[2 + h]
    wait_snapshot(last)
    image(last, 0, nlag)
    for s in range(SNAPS):
        wait_snapshot_sends(s)


def local(
    sizes,
    source_fields,
    receiver_fields,
    courant,
    epsilon,
    delta_param,
    tilt_angle,
    source_pos,
    wavelet,
    receiver_pos,
    receiver_data,
    step_counts,
    offset_lags,
):
    nz, nx, ny = courant.shape
    nlag = offset_lags.shape[0]
    rows = 3 * nx
    f32, bf16 = jnp.float32, jnp.bfloat16
    vmem = pl.BlockSpec(memory_space=pltpu.VMEM)
    smem = pl.BlockSpec(memory_space=pltpu.SMEM)
    images, source_out, receiver_out = pl.pallas_call(
        functools.partial(kernel, sizes),
        out_shape=(
            jax.ShapeDtypeStruct((nlag, nz * nx, ny), bf16),
            jax.ShapeDtypeStruct(source_fields.shape, f32),
            jax.ShapeDtypeStruct(receiver_fields.shape, f32),
        ),
        in_specs=[vmem] * 6 + [smem] * 2 + [vmem] * 2 + [smem] * 2,
        out_specs=(vmem, vmem, vmem),
        scratch_shapes=[
            pltpu.VMEM((2, 4, nz + 2, rows, ny), f32),
            pltpu.VMEM((4, nz, nx, ny), f32),
            pltpu.VMEM((2, 2, nz, nx, ny), f32),
            pltpu.VMEM((2, 2, 4, nz, ny), f32),
            pltpu.VMEM((2, 2, 4, nz, ny), f32),
            pltpu.VMEM((2, 4, 8, ny), f32),
            pltpu.VMEM((2, 4, 8, ny), f32),
            pltpu.VMEM((6, nz, nx, ny), f32),
            pltpu.VMEM((SNAPS * STEPS, nz, nx, ny), f32),
            pltpu.VMEM((nz, nx, ny), f32),
            pltpu.VMEM((SNAPS, 2, nz * nx, ny), bf16),
            pltpu.VMEM((SNAPS, 5, 2, nz * nx, ny), bf16),
            pltpu.VMEM((2, nz, rows, ny), f32),
            pltpu.VMEM((2, nz, rows, ny), f32),
            pltpu.VMEM((nlag, nz * nx, ny), f32),
            pltpu.SemaphoreType.DMA((2, 9)),
            pltpu.SemaphoreType.DMA((2, 9)),
            pltpu.SemaphoreType.DMA((SNAPS, 5)),
            pltpu.SemaphoreType.DMA((SNAPS, 5)),
        ],
        compiler_params=pltpu.CompilerParams(
            collective_id=0, has_side_effects=True, vmem_limit_bytes=32 * 1024 * 1024
        ),
    )(
        source_fields,
        receiver_fields,
        courant,
        epsilon,
        delta_param,
        tilt_angle,
        source_pos,
        wavelet,
        receiver_pos.T,
        receiver_data,
        step_counts,
        offset_lags,
    )
    return images.reshape(nlag, nz, nx, ny), source_out, receiver_out


def solution(mesh):
    fields = P("shot", "sec", "gx", "gy")
    grid = P("sec", "gx", "gy")
    sizes = tuple(mesh.shape[axis] for axis in ("gx", "sec", "gy"))
    return jax.shard_map(
        functools.partial(local, sizes),
        mesh=mesh,
        in_specs=(
            fields,
            fields,
            grid,
            grid,
            grid,
            grid,
            P("shot"),
            P("shot"),
            P("shot", None),
            P("shot", None),
            P(),
            P(),
        ),
        out_specs=(fields, fields, fields),
        check_vma=False,
    )
```

```python
import functools

import jax
import jax.numpy as jnp
from jax import lax
from jax.experimental import pallas as pl
from jax.experimental.pallas import tpu as pltpu
from jax.sharding import PartitionSpec as P

SNAPS = 3
STEPS = 3
DEEP = STEPS
MESH = pl.DeviceIdType.MESH

TOP = 8
SIDE = 4
WAYS = ((-1, 0), (1, 0), (0, -1), (0, 1), (-1, -1), (-1, 1), (1, -1), (1, 1))
SNAP_WAYS = ((-1, False), (1, False), (0, True), (-1, True), (1, True))


def layers(dx, dz, depth, nz, nx):
    if dz == 0:
        z_from, z_to, z_count = DEEP, DEEP, nz
    elif dz < 0:
        z_from, z_to, z_count = DEEP, DEEP + nz, depth
    else:
        z_from, z_to, z_count = DEEP + nz - depth, DEEP - depth, depth
    first = TOP + SIDE
    if dx == 0:
        x_from, x_to, x_count = first, first, nx
    elif dx < 0:
        x_from, x_to, x_count = first, first + nx, depth
    else:
        x_from, x_to, x_count = first + nx - depth, first - depth, depth
    return z_from, z_to, z_count, x_from, x_to, x_count


def message_rows(dx, dz, depths, nz, nx):
    total = 0
    for depth in depths:
        _, _, z_count, _, _, x_count = layers(dx, dz, depth, nz, nx)
        total += z_count * x_count
    return -(-total // 8) * 8


FIELD_DEPTHS = (DEEP, DEEP, DEEP - 1, DEEP - 1)
COEF_DEPTHS = (DEEP - 1,) * 4


def kernel(
    sizes,
    src_ref,
    rec_ref,
    cou_ref,
    eps_ref,
    del_ref,
    tilt_ref,
    spos_ref,
    wav_ref,
    rpos_ref,
    rdat_ref,
    cnt_ref,
    lag_ref,
    img_ref,
    so_ref,
    ro_ref,
    *scratch,
):
    now, new, old, raw, coef, dep = scratch[:6]
    mine, theirs, halves = scratch[6:9]
    field_send, field_recv = scratch[9:17], scratch[17:25]
    coef_send, coef_recv = scratch[25:33], scratch[33:41]
    snap_send, snap_recv, centre, beside, acc, both, give = scratch[41:48]
    load_sem, pair_ssem, pair_rsem, halo_ssem, halo_rsem, snap_ssem, snap_rsem = scratch[48:]
    nz, nx, ny = cou_ref.shape
    nlag = lag_ref.shape[1]
    window = nx + 2 * SIDE
    first = TOP + SIDE
    rows = slice(TOP, TOP + window)
    block = slice(first, first + nx)
    ngx, nsec, _ = sizes
    gx, sec, gy = lax.axis_index("gx"), lax.axis_index("sec"), lax.axis_index("gy")
    is_source = gy == 0

    def exists(dx, dz):
        ok = None
        if dx:
            ok = gx > 0 if dx < 0 else gx < ngx - 1
        if dz:
            okz = sec > 0 if dz < 0 else sec < nsec - 1
            ok = okz if ok is None else jnp.logical_and(ok, okz)
        return ok

    def guarded(ok, action):
        if ok is None:
            action()
        else:
            pl.when(ok)(action)

    def device(dx, dz, other):
        where = {}
        if dx:
            where["gx"] = gx + dx
        if dz:
            where["sec"] = sec + dz
        if other:
            where["gy"] = 1 - gy
        return where

    def remote(src, dst, send_sem, recv_sem, where):
        return pltpu.make_async_remote_copy(
            src_ref=src,
            dst_ref=dst,
            send_sem=send_sem,
            recv_sem=recv_sem,
            device_id=where,
            device_id_type=MESH,
        )

    coef_refs = (cou_ref, eps_ref, del_ref, tilt_ref)
    loads = [
        pltpu.make_async_copy(ref, halves.at[0, i], load_sem.at[i])
        for i, ref in enumerate(coef_refs)
    ]
    for copy in loads:
        copy.start()
    load_source = pltpu.make_async_copy(src_ref, mine, load_sem.at[4])
    load_receiver = pltpu.make_async_copy(rec_ref, mine, load_sem.at[4])
    pl.when(is_source)(load_source.start)
    pl.when(jnp.logical_not(is_source))(load_receiver.start)

    barrier = pltpu.get_barrier_semaphore()
    total = jnp.int32(1)
    pl.semaphore_signal(barrier, inc=1, device_id=device(0, 0, True), device_id_type=MESH)
    for dx, dz, other in [(dx, dz, False) for dx, dz in WAYS] + [(-1, 0, True), (1, 0, True)]:
        ok = exists(dx, dz)
        total = total + ok.astype(jnp.int32)

        @pl.when(ok)
        def _():
            pl.semaphore_signal(
                barrier, inc=1, device_id=device(dx, dz, other), device_id_type=MESH
            )

    for ref in (now, old, raw):
        ref[:, :, rows, :] = jnp.zeros((ref.shape[0], ref.shape[1], window, 2 * ny), jnp.float32)
    centre[...] = jnp.zeros_like(centre)
    beside[...] = jnp.zeros_like(beside)
    pl.semaphore_wait(barrier, total)

    pairs = [
        remote(ref, halves.at[1, i], pair_ssem.at[i], pair_rsem.at[i], device(0, 0, True))
        for i, ref in enumerate(coef_refs)
    ]
    to_pair = device(0, 0, True)
    swap_receiver = remote(rec_ref, theirs, pair_ssem.at[4], pair_rsem.at[4], to_pair)
    swap_source = remote(src_ref, theirs, pair_ssem.at[4], pair_rsem.at[4], to_pair)
    for copy in pairs:
        copy.start()
    pl.when(is_source)(swap_receiver.start)
    pl.when(jnp.logical_not(is_source))(swap_source.start)

    def joined(own, other):
        left = jnp.where(is_source, own, other)
        right = jnp.where(is_source, other, own)
        return left, right

    def split(whole):
        left, right = whole[..., :ny], whole[..., ny:]
        return jnp.where(is_source, left, right), jnp.where(is_source, right, left)

    def pack(buffer, arrays, depths, dx, dz):
        at = 0
        for (ref, f), depth in zip(arrays, depths):
            z_from, _, z_count, x_from, _, x_count = layers(dx, dz, depth, nz, nx)
            for z in range(z_count):
                buffer[at : at + x_count, :] = ref[f, z_from + z, x_from : x_from + x_count, :]
                at += x_count

    def unpack(buffer, arrays, depths, dx, dz):
        at = 0
        for (ref, f), depth in zip(arrays, depths):
            _, z_to, z_count, _, x_to, x_count = layers(dx, dz, depth, nz, nx)
            for z in range(z_count):
                ref[f, z_to + z, x_to : x_to + x_count, :] = buffer[at : at + x_count, :]
                at += x_count

    coef_arrays = [(raw, i) for i in range(4)]
    field_arrays = [(now, 0), (now, 1), (old, 0), (old, 1)]

    def coef_copy(n):
        return remote(
            coef_send[n],
            coef_recv[n],
            halo_ssem.at[SNAPS, n],
            halo_rsem.at[SNAPS, n],
            device(*WAYS[n], False),
        )

    def field_copy(s, n):
        return remote(
            field_send[n].at[s],
            field_recv[n].at[s],
            halo_ssem.at[s, n],
            halo_rsem.at[s, n],
            device(*WAYS[n], False),
        )

    def send_fields(s):
        for n, (dx, dz) in enumerate(WAYS):

            def go():
                pack(field_send[n].at[s], field_arrays, FIELD_DEPTHS, dx, dz)
                field_copy(s, n).start()

            guarded(exists(dx, dz), go)

    def take_fields(s):
        for n, (dx, dz) in enumerate(WAYS):

            def go():
                field_copy(s, n).wait_recv()
                unpack(field_recv[n].at[s], field_arrays, FIELD_DEPTHS, dx, dz)

            guarded(exists(-dx, -dz), go)

    for copy in loads:
        copy.wait()
    load_source.wait()
    for copy in pairs:
        copy.wait_recv()
    swap_source.wait_recv()
    for ref, f, own, other in [
        (raw, i, halves.at[0, i], halves.at[1, i]) for i in range(4)
    ] + [(ref, f, mine.at[i], theirs.at[i]) for i, (ref, f) in enumerate(field_arrays)]:
        left, right = joined(own[...], other[...])
        ref[f, DEEP : DEEP + nz, block, :ny] = left
        ref[f, DEEP : DEEP + nz, block, ny:] = right

    for n, (dx, dz) in enumerate(WAYS):

        def go():
            pack(coef_send[n], coef_arrays, COEF_DEPTHS, dx, dz)
            coef_copy(n).start()

        guarded(exists(dx, dz), go)

    def deposits():
        nrec = rpos_ref.shape[1]
        lane = lax.broadcasted_iota(jnp.int32, (1, nrec), 1)

        def points(d):
            alone = jnp.where(lane == 0, spos_ref[d], -1)
            return jnp.where(is_source, alone, rpos_ref[d : d + 1, :])

        planes = nz + 2 * (DEEP - 1)
        pz = points(0) - sec * nz + (DEEP - 1)
        px = points(1) - gx * nx + SIDE
        py = points(2)
        at_y = lax.broadcasted_iota(jnp.int32, (2 * ny, nrec), 0) == py
        at_y = jnp.where(at_y, 1.0, 0.0).astype(jnp.bfloat16)
        cell = jnp.where((px >= 0) & (px < window), pz * window + px, -1)
        at_cell = lax.broadcasted_iota(jnp.int32, (planes * window, nrec), 0) == cell

        def slot(t, carry):
            alone = jnp.where(lane == 0, wav_ref[t], 0.0)
            left = jnp.where(is_source, alone, rdat_ref[pl.ds(t, 1), :])
            summed = jnp.zeros((planes * window, 2 * ny), jnp.float32)
            for _ in range(3):
                part = left.astype(jnp.bfloat16).astype(jnp.float32)
                left = left - part
                picked = jnp.where(at_cell, part, 0.0).astype(jnp.bfloat16)
                summed = summed + lax.dot_general(
                    picked, at_y, (((1,), (1,)), ((), ())), preferred_element_type=jnp.float32
                )
            dep[t] = summed.reshape(planes, window, 2 * ny)
            return carry

        lax.fori_loop(0, SNAPS * STEPS, slot, 0)

    def coefficients():
        for n, (dx, dz) in enumerate(WAYS):

            def go():
                coef_copy(n).wait_recv()
                unpack(coef_recv[n], coef_arrays, COEF_DEPTHS, dx, dz)

            guarded(exists(-dx, -dz), go)

        def plane(z, carry):
            tilt = raw[3, 1 + z, rows, :]
            cos_tilt, sin_tilt = jnp.cos(tilt), jnp.sin(tilt)
            coef[0, z] = raw[0, 1 + z, rows, :]
            coef[1, z] = 1.0 + 2.0 * raw[1, 1 + z, rows, :]
            coef[2, z] = 1.0 + 2.0 * raw[2, 1 + z, rows, :]
            coef[3, z] = cos_tilt * cos_tilt
            coef[4, z] = sin_tilt * sin_tilt
            coef[5, z] = 2.0 * sin_tilt * cos_tilt
            return carry

        lax.fori_loop(0, nz + 2 * (DEEP - 1), plane, 0)

    def snap_copy(s, n):
        dx, other = SNAP_WAYS[n]
        return remote(
            snap_send.at[s],
            snap_recv.at[s, n],
            snap_ssem.at[s, n],
            snap_rsem.at[s, n],
            device(dx, 0, other),
        )

    lane = lax.broadcasted_iota(jnp.int32, (nx, ny), 1)
    keep = (lane < ny // 2) == is_source

    def place(s, section, dx, whole):
        start = nx - dx * nx
        own, other = split(whole.astype(jnp.float32).reshape(nz, nx, 2 * ny))
        centre[s, section, :, start : start + nx, :] = own
        beside[s, section, :, start : start + nx, :] = jnp.where(keep[None], other, 0.0)

    def send_snapshot(s, ref):
        rounded = ref[0, DEEP : DEEP + nz, block, :].astype(jnp.bfloat16)
        rounded = rounded.reshape(nz * nx, 2 * ny)
        snap_send[s] = rounded
        for n, (dx, other) in enumerate(SNAP_WAYS):
            guarded(exists(dx, 0), snap_copy(s, n).start)
        place(s, gy, 0, rounded)

    def take_snapshot(s):
        for n, (dx, other) in enumerate(SNAP_WAYS):

            def go():
                snap_copy(s, n).wait_recv()
                place(s, 1 - gy if other else gy, dx, snap_recv[s, n])

            guarded(exists(-dx, 0), go)

    def image(s):
        def one_lag(lag, carry):
            lx = lag_ref[0, lag]
            ly = lag_ref[1, lag]

            def shifted(h, sx, sy):
                c = centre[s, h, :, pl.ds(nx + sx, nx), :]
                b = beside[s, h, :, pl.ds(nx + sx, nx), :]
                edge = jnp.logical_or(lane < sy, lane >= ny + sy)
                mixed = jnp.where(edge[None], b, c)
                return pltpu.roll(mixed, lax.rem(ny - sy, ny), 2)

            product = shifted(0, -lx, -ly) * shifted(1, lx, ly)
            product = product.reshape(nz * nx, ny)
            if s == 0:
                acc[lag] = product
            elif s < SNAPS - 1:
                acc[lag] = acc[lag] + product
            else:
                img_ref[lag] = (acc[lag] + product).astype(jnp.bfloat16)
            return carry

        lax.fori_loop(0, nlag, one_lag, 0)

    wide_lane = lax.broadcasted_iota(jnp.int32, (window, 2 * ny), 1)
    first_lane = wide_lane == 0
    last_lane = wide_lane == 2 * ny - 1

    def advance(k, halo, active, here, there):
        for z in range(DEEP - halo, DEEP + nz + halo):
            c = z - 1

            def diffs(f):
                def at(dz, dx):
                    return here[f, z + dz, TOP + dx : TOP + window + dx, :]

                mid = at(0, 0)
                zz = at(1, 0) + at(-1, 0) - 2.0 * mid
                xx = at(0, 1) + at(0, -1) - 2.0 * mid
                xz = 0.25 * (at(1, 1) - at(1, -1) - at(-1, 1) + at(-1, -1))
                return mid, zz, xx, xz

            p, pzz, pxx, pxz = diffs(0)
            q, qzz, qxx, qxz = diffs(1)
            above = jnp.where(last_lane, 0.0, pltpu.roll(p, 2 * ny - 1, 1))
            below = jnp.where(first_lane, 0.0, pltpu.roll(p, 1, 1))
            pyy = above + below - 2.0 * p
            wz, wx, wm = coef[3, c], coef[4, c], coef[5, c]
            vert_p = wz * pzz + wx * pxx + wm * pxz
            horiz = pzz + pxx + pyy - vert_p
            vert_q = wz * qzz + wx * qxx + wm * qxz
            p_old, q_old = old[0, z, rows, :], old[1, z, rows, :]
            amount = dep[k, c]
            cou = coef[0, c]
            new_p = 2.0 * p - p_old + cou * (coef[1, c] * horiz + vert_q) + amount
            new_q = 2.0 * q - q_old + cou * (coef[2, c] * horiz + vert_q) + amount
            there[0, z, rows, :] = jnp.where(active, new_p, p)
            there[1, z, rows, :] = jnp.where(active, new_q, q)
            old[0, z, rows, :] = jnp.where(active, p, p_old)
            old[1, z, rows, :] = jnp.where(active, q, q_old)

    def window_steps(s, carry):
        send_fields(s)

        @pl.when(s == 0)
        def _():
            deposits()
            coefficients()

        @pl.when(s > 0)
        def _():
            send_snapshot(s - 1, now)

        @pl.when(s == SNAPS - 1)
        def _():
            take_snapshot(0)
            image(0)

        take_fields(s)
        here, there = now, new
        for j in range(STEPS):
            advance(s * STEPS + j, STEPS - 1 - j, j < cnt_ref[s], here, there)
            here, there = there, here
        if here is new:
            for f in range(2):
                now[f, DEEP : DEEP + nz, rows, :] = new[f, DEEP : DEEP + nz, rows, :]
        return carry

    lax.fori_loop(0, SNAPS, window_steps, 0)

    send_snapshot(SNAPS - 1, now)
    for i, (ref, f) in enumerate(field_arrays):
        own, other = split(ref[f, DEEP : DEEP + nz, block, :])
        both[gy, i] = own
        give[i] = other
    back = remote(give, both.at[gy], pair_ssem.at[5], pair_rsem.at[5], to_pair)
    back.start()
    for s in range(1, SNAPS - 1):
        take_snapshot(s)
        image(s)
    take_snapshot(SNAPS - 1)
    image(SNAPS - 1)
    remote(give, both.at[1 - gy], pair_ssem.at[5], pair_rsem.at[5], to_pair).wait_recv()
    so_ref[...] = both[0]
    ro_ref[...] = both[1]

    back.wait_send()
    for copy in pairs:
        copy.wait_send()
    swap_source.wait_send()
    for n, (dx, dz) in enumerate(WAYS):

        def ended():
            coef_copy(n).wait_send()
            for s in range(SNAPS):
                field_copy(s, n).wait_send()

        guarded(exists(dx, dz), ended)
    for n, (dx, _) in enumerate(SNAP_WAYS):

        def ended():
            for s in range(SNAPS):
                snap_copy(s, n).wait_send()

        guarded(exists(dx, 0), ended)


def local(
    sizes,
    source_fields,
    receiver_fields,
    courant,
    epsilon,
    delta_param,
    tilt_angle,
    source_pos,
    wavelet,
    receiver_pos,
    receiver_data,
    step_counts,
    offset_lags,
):
    nz, nx, ny = courant.shape
    nlag = offset_lags.shape[0]
    f32, bf16 = jnp.float32, jnp.bfloat16
    vmem = pl.BlockSpec(memory_space=pltpu.VMEM)
    smem = pl.BlockSpec(memory_space=pltpu.SMEM)
    hbm = pl.BlockSpec(memory_space=pltpu.HBM)
    wide = 2 * ny
    window = nx + 2 * SIDE
    whole = (nz + 2 * DEEP, window + 2 * TOP, wide)
    inner = (nz + 2 * (DEEP - 1), window, wide)
    field_rows = [message_rows(dx, dz, FIELD_DEPTHS, nz, nx) for dx, dz in WAYS]
    coef_rows = [message_rows(dx, dz, COEF_DEPTHS, nz, nx) for dx, dz in WAYS]
    images, source_out, receiver_out = pl.pallas_call(
        functools.partial(kernel, sizes),
        out_shape=(
            jax.ShapeDtypeStruct((nlag, nz * nx, ny), bf16),
            jax.ShapeDtypeStruct(source_fields.shape, f32),
            jax.ShapeDtypeStruct(receiver_fields.shape, f32),
        ),
        in_specs=[hbm] * 6 + [smem] * 2 + [vmem] * 2 + [smem] * 2,
        out_specs=(vmem, vmem, vmem),
        scratch_shapes=[
            pltpu.VMEM((2, *whole), f32),
            pltpu.VMEM((2, *whole), f32),
            pltpu.VMEM((2, *whole), f32),
            pltpu.VMEM((4, *whole), f32),
            pltpu.VMEM((6, *inner), f32),
            pltpu.VMEM((SNAPS * STEPS, *inner), f32),
            pltpu.VMEM((4, nz, nx, ny), f32),
            pltpu.VMEM((4, nz, nx, ny), f32),
            pltpu.VMEM((2, 4, nz, nx, ny), f32),
            *[pltpu.VMEM((SNAPS, count, wide), f32) for count in field_rows * 2],
            *[pltpu.VMEM((count, wide), f32) for count in coef_rows * 2],
            pltpu.VMEM((SNAPS, nz * nx, wide), bf16),
            pltpu.VMEM((SNAPS, len(SNAP_WAYS), nz * nx, wide), bf16),
            pltpu.VMEM((SNAPS, 2, nz, 3 * nx, ny), f32),
            pltpu.VMEM((SNAPS, 2, nz, 3 * nx, ny), f32),
            pltpu.VMEM((nlag, nz * nx, ny), f32),
            pltpu.VMEM((2, 4, nz, nx, ny), f32),
            pltpu.VMEM((4, nz, nx, ny), f32),
            pltpu.SemaphoreType.DMA((5,)),
            pltpu.SemaphoreType.DMA((6,)),
            pltpu.SemaphoreType.DMA((6,)),
            pltpu.SemaphoreType.DMA((SNAPS + 1, len(WAYS))),
            pltpu.SemaphoreType.DMA((SNAPS + 1, len(WAYS))),
            pltpu.SemaphoreType.DMA((SNAPS, len(SNAP_WAYS))),
            pltpu.SemaphoreType.DMA((SNAPS, len(SNAP_WAYS))),
        ],
        compiler_params=pltpu.CompilerParams(
            collective_id=0, has_side_effects=True, vmem_limit_bytes=48 * 1024 * 1024
        ),
    )(
        source_fields,
        receiver_fields,
        courant,
        epsilon,
        delta_param,
        tilt_angle,
        source_pos,
        wavelet,
        receiver_pos.T,
        receiver_data,
        step_counts,
        offset_lags.T,
    )
    return images.reshape(nlag, nz, nx, ny), source_out, receiver_out


def solution(mesh):
    fields = P("shot", "sec", "gx", "gy")
    grid = P("sec", "gx", "gy")
    sizes = tuple(mesh.shape[axis] for axis in ("gx", "sec", "gy"))
    return jax.shard_map(
        functools.partial(local, sizes),
        mesh=mesh,
        in_specs=(
            fields,
            fields,
            grid,
            grid,
            grid,
            grid,
            P("shot"),
            P("shot"),
            P("shot", None),
            P("shot", None),
            P(),
            P(),
        ),
        out_specs=(fields, fields, fields),
        check_vma=False,
    )
```

```python
import functools

import jax
import jax.numpy as jnp
from jax import lax
from jax.experimental import pallas as pl
from jax.experimental.pallas import tpu as pltpu
from jax.sharding import PartitionSpec as P

SNAPS = 3
STEPS = 3
DEEP = STEPS
MESH = pl.DeviceIdType.MESH

TOP = 8
SIDE = 4
WAYS = ((-1, 0), (1, 0), (0, -1), (0, 1), (-1, -1), (-1, 1), (1, -1), (1, 1))
SNAP_WAYS = ((-1, False), (1, False), (0, True), (-1, True), (1, True))


def layers(dx, dz, depth, nz, nx):
    if dz == 0:
        z_from, z_to, z_count = DEEP, DEEP, nz
    elif dz < 0:
        z_from, z_to, z_count = DEEP, DEEP + nz, depth
    else:
        z_from, z_to, z_count = DEEP + nz - depth, DEEP - depth, depth
    first = TOP + SIDE
    if dx == 0:
        x_from, x_to, x_count = first, first, nx
    elif dx < 0:
        x_from, x_to, x_count = first, first + nx, depth
    else:
        x_from, x_to, x_count = first + nx - depth, first - depth, depth
    return z_from, z_to, z_count, x_from, x_to, x_count


def message_rows(dx, dz, depths, nz, nx):
    total = 0
    for depth in depths:
        _, _, z_count, _, _, x_count = layers(dx, dz, depth, nz, nx)
        total += z_count * x_count
    return -(-total // 8) * 8


FIELD_DEPTHS = (DEEP, DEEP, DEEP - 1, DEEP - 1)
COEF_DEPTHS = (DEEP - 1,) * 4


def kernel(
    sizes,
    src_ref,
    rec_ref,
    cou_ref,
    eps_ref,
    del_ref,
    tilt_ref,
    spos_ref,
    wav_ref,
    rpos_ref,
    rdat_ref,
    cnt_ref,
    lag_ref,
    img_ref,
    so_ref,
    ro_ref,
    *scratch,
):
    small_hbm = (spos_ref, wav_ref, cnt_ref, lag_ref, rpos_ref, rdat_ref)
    small = scratch[-6:]
    spos_ref, wav_ref, cnt_ref, lag_ref, rpos_ref, rdat_ref = small
    scratch = scratch[:-6]
    now, new, old, raw, coef, dep = scratch[:6]
    mine, theirs, halves = scratch[6:9]
    field_send, field_recv = scratch[9:17], scratch[17:25]
    coef_send, coef_recv = scratch[25:33], scratch[33:41]
    snap_send, snap_recv, centre, beside, acc, both, give = scratch[41:48]
    load_sem, pair_ssem, pair_rsem, halo_ssem, halo_rsem, snap_ssem, snap_rsem = scratch[48:]
    nz, nx, ny = cou_ref.shape
    nlag = lag_ref.shape[1]
    window = nx + 2 * SIDE
    first = TOP + SIDE
    rows = slice(TOP, TOP + window)
    block = slice(first, first + nx)
    ngx, nsec, _ = sizes
    gx, sec, gy = lax.axis_index("gx"), lax.axis_index("sec"), lax.axis_index("gy")
    is_source = gy == 0

    def exists(dx, dz):
        ok = None
        if dx:
            ok = gx > 0 if dx < 0 else gx < ngx - 1
        if dz:
            okz = sec > 0 if dz < 0 else sec < nsec - 1
            ok = okz if ok is None else jnp.logical_and(ok, okz)
        return ok

    def guarded(ok, action):
        if ok is None:
            action()
        else:
            pl.when(ok)(action)

    def device(dx, dz, other):
        where = {}
        if dx:
            where["gx"] = gx + dx
        if dz:
            where["sec"] = sec + dz
        if other:
            where["gy"] = 1 - gy
        return where

    def remote(src, dst, send_sem, recv_sem, where):
        return pltpu.make_async_remote_copy(
            src_ref=src,
            dst_ref=dst,
            send_sem=send_sem,
            recv_sem=recv_sem,
            device_id=where,
            device_id_type=MESH,
        )

    coef_refs = (cou_ref, eps_ref, del_ref, tilt_ref)
    loads = [
        pltpu.make_async_copy(ref, halves.at[0, i], load_sem.at[i])
        for i, ref in enumerate(coef_refs)
    ]
    loads += [
        pltpu.make_async_copy(ref, held, load_sem.at[5 + i])
        for i, (ref, held) in enumerate(zip(small_hbm, small))
    ]
    for copy in loads:
        copy.start()
    load_source = pltpu.make_async_copy(src_ref, mine, load_sem.at[4])
    load_receiver = pltpu.make_async_copy(rec_ref, mine, load_sem.at[4])
    pl.when(is_source)(load_source.start)
    pl.when(jnp.logical_not(is_source))(load_receiver.start)

    barrier = pltpu.get_barrier_semaphore()
    total = jnp.int32(1)
    pl.semaphore_signal(barrier, inc=1, device_id=device(0, 0, True), device_id_type=MESH)
    for dx, dz, other in [(dx, dz, False) for dx, dz in WAYS] + [(-1, 0, True), (1, 0, True)]:
        ok = exists(dx, dz)
        total = total + ok.astype(jnp.int32)

        @pl.when(ok)
        def _():
            pl.semaphore_signal(
                barrier, inc=1, device_id=device(dx, dz, other), device_id_type=MESH
            )

    for ref in (now, old, raw):
        ref[:, :, :, rows, :] = jnp.zeros(ref.shape[:3] + (window, ny), jnp.float32)
    centre[...] = jnp.zeros_like(centre)
    beside[...] = jnp.zeros_like(beside)
    pl.semaphore_wait(barrier, total)

    pairs = [
        remote(ref, halves.at[1, i], pair_ssem.at[i], pair_rsem.at[i], device(0, 0, True))
        for i, ref in enumerate(coef_refs)
    ]
    to_pair = device(0, 0, True)
    swap_receiver = remote(rec_ref, theirs, pair_ssem.at[4], pair_rsem.at[4], to_pair)
    swap_source = remote(src_ref, theirs, pair_ssem.at[4], pair_rsem.at[4], to_pair)
    for copy in pairs:
        copy.start()
    pl.when(is_source)(swap_receiver.start)
    pl.when(jnp.logical_not(is_source))(swap_source.start)

    def joined(own, other):
        left = jnp.where(is_source, own, other)
        right = jnp.where(is_source, other, own)
        return left, right

    def split(left, right):
        return jnp.where(is_source, left, right), jnp.where(is_source, right, left)

    def pack(buffer, arrays, depths, dx, dz):
        at = 0
        for (ref, f), depth in zip(arrays, depths):
            z_from, _, z_count, x_from, _, x_count = layers(dx, dz, depth, nz, nx)
            for z in range(z_count):
                buffer[:, at : at + x_count, :] = ref[f, z_from + z, :, x_from : x_from + x_count, :]
                at += x_count

    def unpack(buffer, arrays, depths, dx, dz):
        at = 0
        for (ref, f), depth in zip(arrays, depths):
            _, z_to, z_count, _, x_to, x_count = layers(dx, dz, depth, nz, nx)
            for z in range(z_count):
                ref[f, z_to + z, :, x_to : x_to + x_count, :] = buffer[:, at : at + x_count, :]
                at += x_count

    coef_arrays = [(raw, i) for i in range(4)]
    field_arrays = [(now, 0), (now, 1), (old, 0), (old, 1)]

    def coef_copy(n):
        return remote(
            coef_send[n],
            coef_recv[n],
            halo_ssem.at[SNAPS, n],
            halo_rsem.at[SNAPS, n],
            device(*WAYS[n], False),
        )

    def field_copy(s, n):
        return remote(
            field_send[n].at[s],
            field_recv[n].at[s],
            halo_ssem.at[s, n],
            halo_rsem.at[s, n],
            device(*WAYS[n], False),
        )

    def send_fields(s):
        for n, (dx, dz) in enumerate(WAYS):

            def go():
                pack(field_send[n].at[s], field_arrays, FIELD_DEPTHS, dx, dz)
                field_copy(s, n).start()

            guarded(exists(dx, dz), go)

    def take_fields(s):
        for n, (dx, dz) in enumerate(WAYS):

            def go():
                field_copy(s, n).wait_recv()
                unpack(field_recv[n].at[s], field_arrays, FIELD_DEPTHS, dx, dz)

            guarded(exists(-dx, -dz), go)

    for copy in loads:
        copy.wait()
    load_source.wait()
    for copy in pairs:
        copy.wait_recv()
    swap_source.wait_recv()
    for ref, f, own, other in [
        (raw, i, halves.at[0, i], halves.at[1, i]) for i in range(4)
    ] + [(ref, f, mine.at[i], theirs.at[i]) for i, (ref, f) in enumerate(field_arrays)]:
        left, right = joined(own[...], other[...])
        ref[f, DEEP : DEEP + nz, 0, block, :] = left
        ref[f, DEEP : DEEP + nz, 1, block, :] = right

    for n, (dx, dz) in enumerate(WAYS):

        def go():
            pack(coef_send[n], coef_arrays, COEF_DEPTHS, dx, dz)
            coef_copy(n).start()

        guarded(exists(dx, dz), go)

    planes = nz + 2 * (DEEP - 1)

    def deposits(s):
        nrec = rpos_ref.shape[1]
        lane = lax.broadcasted_iota(jnp.int32, (1, nrec), 1)

        def points(d):
            alone = jnp.where(lane == 0, spos_ref[d], -1)
            return jnp.where(is_source, alone, rpos_ref[d : d + 1, :])

        pz = points(0) - sec * nz + (DEEP - 1)
        px = points(1) - gx * nx + SIDE
        py = points(2)
        at_y = lax.broadcasted_iota(jnp.int32, (2 * ny, nrec), 0) == py
        at_y = jnp.where(at_y, 1.0, 0.0).astype(jnp.bfloat16)
        cell = jnp.where((px >= 0) & (px < window), pz * window + px, -1)
        at_cell = lax.broadcasted_iota(jnp.int32, (planes * window, nrec), 0) == cell
        for j in range(STEPS):
            t = s * STEPS + j
            alone = jnp.where(lane == 0, wav_ref[t], 0.0)
            amounts = jnp.where(is_source, alone, rdat_ref[pl.ds(t, 1), :])
            high = amounts.astype(jnp.bfloat16).astype(jnp.float32)
            summed = None
            for part in (high, amounts - high):
                picked = jnp.where(at_cell, part, 0.0).astype(jnp.bfloat16)
                term = lax.dot_general(
                    picked, at_y, (((1,), (1,)), ((), ())), preferred_element_type=jnp.float32
                )
                summed = term if summed is None else summed + term
            for half in range(2):
                lanes = summed[:, half * ny : (half + 1) * ny]
                dep[j, :, half] = lanes.reshape(planes, window, ny)

    def coefficients():
        for n, (dx, dz) in enumerate(WAYS):

            def go():
                coef_copy(n).wait_recv()
                unpack(coef_recv[n], coef_arrays, COEF_DEPTHS, dx, dz)

            guarded(exists(-dx, -dz), go)

        def plane(z, carry):
            tilt = raw[3, 1 + z, :, rows, :]
            cos_tilt, sin_tilt = jnp.cos(tilt), jnp.sin(tilt)
            coef[0, z] = raw[0, 1 + z, :, rows, :]
            coef[1, z] = 1.0 + 2.0 * raw[1, 1 + z, :, rows, :]
            coef[2, z] = 1.0 + 2.0 * raw[2, 1 + z, :, rows, :]
            coef[3, z] = cos_tilt * cos_tilt
            coef[4, z] = sin_tilt * sin_tilt
            coef[5, z] = 0.5 * sin_tilt * cos_tilt
            return carry

        lax.fori_loop(0, planes, plane, 0)

    def snap_copy(s, n):
        dx, other = SNAP_WAYS[n]
        return remote(
            snap_send.at[s],
            snap_recv.at[s, n],
            snap_ssem.at[s, n],
            snap_rsem.at[s, n],
            device(dx, 0, other),
        )

    lane = lax.broadcasted_iota(jnp.int32, (nx, ny), 1)
    keep = (lane < ny // 2) == is_source

    def place(s, section, dx, whole):
        start = nx - dx * nx
        whole = whole.astype(jnp.float32)
        own, other = split(whole[0].reshape(nz, nx, ny), whole[1].reshape(nz, nx, ny))
        centre[s, section, :, start : start + nx, :] = own
        beside[s, section, :, start : start + nx, :] = jnp.where(keep[None], other, 0.0)

    def send_snapshot(s, ref):
        for half in range(2):
            rounded = ref[0, DEEP : DEEP + nz, half, block, :].astype(jnp.bfloat16)
            snap_send[s, half] = rounded.reshape(nz * nx, ny)
        for n, (dx, other) in enumerate(SNAP_WAYS):
            guarded(exists(dx, 0), snap_copy(s, n).start)
        place(s, gy, 0, snap_send[s])

    def take_snapshot(s):
        for n, (dx, other) in enumerate(SNAP_WAYS):

            def go():
                snap_copy(s, n).wait_recv()
                place(s, 1 - gy if other else gy, dx, snap_recv[s, n])

            guarded(exists(-dx, 0), go)

    def image(s):
        def one_lag(lag, carry):
            lx = lag_ref[0, lag]
            ly = lag_ref[1, lag]

            def shifted(h, sx, sy):
                c = centre[s, h, :, pl.ds(nx + sx, nx), :]
                b = beside[s, h, :, pl.ds(nx + sx, nx), :]
                edge = jnp.logical_or(lane < sy, lane >= ny + sy)
                mixed = jnp.where(edge[None], b, c)
                return pltpu.roll(mixed, lax.rem(ny - sy, ny), 2)

            product = shifted(0, -lx, -ly) * shifted(1, lx, ly)
            product = product.reshape(nz * nx, ny)
            if s == 0:
                acc[lag] = product
            elif s < SNAPS - 1:
                acc[lag] = acc[lag] + product
            else:
                img_ref[lag] = (acc[lag] + product).astype(jnp.bfloat16)
            return carry

        some = 4 if nlag % 4 == 0 else 1

        def lags(i, carry):
            for more in range(some):
                one_lag(i * some + more, carry)
            return carry

        lax.fori_loop(0, nlag // some, lags, 0)

    step_lane = lax.broadcasted_iota(jnp.int32, (window, ny), 1)
    first_lane = step_lane == 0
    last_lane = step_lane == ny - 1

    def advance(j, halo, active, here, there):
        for z in range(DEEP - halo, DEEP + nz + halo):
            c = z - 1
            left, right = here[0, z, 0, rows, :], here[0, z, 1, rows, :]
            left_up, right_up = pltpu.roll(left, ny - 1, 1), pltpu.roll(right, ny - 1, 1)
            left_down, right_down = pltpu.roll(left, 1, 1), pltpu.roll(right, 1, 1)
            sides = (
                jnp.where(last_lane, right_up, left_up) + jnp.where(first_lane, 0.0, left_down),
                jnp.where(last_lane, 0.0, right_up) + jnp.where(first_lane, left_down, right_down),
            )
            for half in range(2):

                def diffs(f):
                    def at(dz, dx):
                        return here[f, z + dz, half, TOP + dx : TOP + window + dx, :]

                    mid = at(0, 0)
                    twice = 2.0 * mid
                    zz = at(1, 0) + at(-1, 0) - twice
                    xx = at(0, 1) + at(0, -1) - twice
                    xz = at(1, 1) - at(1, -1) - at(-1, 1) + at(-1, -1)
                    return mid, twice, zz, xx, xz

                p, twice_p, pzz, pxx, pxz = diffs(0)
                q, twice_q, qzz, qxx, qxz = diffs(1)
                pyy = sides[half] - twice_p
                wz, wx, wm = coef[3, c, half], coef[4, c, half], coef[5, c, half]
                vert_p = wz * pzz + wx * pxx + wm * pxz
                horiz = pzz + pxx + pyy - vert_p
                vert_q = wz * qzz + wx * qxx + wm * qxz
                p_old, q_old = old[0, z, half, rows, :], old[1, z, half, rows, :]
                amount = dep[j, c, half]
                cou = coef[0, c, half]
                new_p = twice_p - p_old + cou * (coef[1, c, half] * horiz + vert_q) + amount
                new_q = twice_q - q_old + cou * (coef[2, c, half] * horiz + vert_q) + amount
                there[0, z, half, rows, :] = jnp.where(active, new_p, p)
                there[1, z, half, rows, :] = jnp.where(active, new_q, q)
                old[0, z, half, rows, :] = jnp.where(active, p, p_old)
                old[1, z, half, rows, :] = jnp.where(active, q, q_old)

    def window_steps(s, carry):
        send_fields(s)

        @pl.when(s > 0)
        def _():
            send_snapshot(s - 1, now)

        deposits(s)
        pl.when(s == 0)(coefficients)

        @pl.when(s == SNAPS - 1)
        def _():
            take_snapshot(0)
            image(0)

        take_fields(s)
        here, there = now, new
        for j in range(STEPS):
            advance(j, STEPS - 1 - j, j < cnt_ref[s], here, there)
            here, there = there, here
        if here is new:
            for f in range(2):
                now[f, DEEP : DEEP + nz, :, rows, :] = new[f, DEEP : DEEP + nz, :, rows, :]
        return carry

    lax.fori_loop(0, SNAPS, window_steps, 0)

    send_snapshot(SNAPS - 1, now)
    for i, (ref, f) in enumerate(field_arrays):
        own, other = split(
            ref[f, DEEP : DEEP + nz, 0, block, :], ref[f, DEEP : DEEP + nz, 1, block, :]
        )
        both[gy, i] = own
        give[i] = other
    back = remote(give, both.at[gy], pair_ssem.at[5], pair_rsem.at[5], to_pair)
    back.start()
    for s in range(1, SNAPS - 1):
        take_snapshot(s)
        image(s)
    take_snapshot(SNAPS - 1)
    image(SNAPS - 1)
    remote(give, both.at[1 - gy], pair_ssem.at[5], pair_rsem.at[5], to_pair).wait_recv()
    so_ref[...] = both[0]
    ro_ref[...] = both[1]

    back.wait_send()
    for copy in pairs:
        copy.wait_send()
    swap_source.wait_send()
    for n, (dx, dz) in enumerate(WAYS):

        def ended():
            coef_copy(n).wait_send()
            for s in range(SNAPS):
                field_copy(s, n).wait_send()

        guarded(exists(dx, dz), ended)
    for n, (dx, _) in enumerate(SNAP_WAYS):

        def ended():
            for s in range(SNAPS):
                snap_copy(s, n).wait_send()

        guarded(exists(dx, 0), ended)


def local(
    sizes,
    source_fields,
    receiver_fields,
    courant,
    epsilon,
    delta_param,
    tilt_angle,
    source_pos,
    wavelet,
    receiver_pos,
    receiver_data,
    step_counts,
    offset_lags,
):
    nz, nx, ny = courant.shape
    nlag = offset_lags.shape[0]
    f32, bf16 = jnp.float32, jnp.bfloat16
    vmem = pl.BlockSpec(memory_space=pltpu.VMEM)
    hbm = pl.BlockSpec(memory_space=pltpu.HBM)
    window = nx + 2 * SIDE
    whole = (nz + 2 * DEEP, 2, window + 2 * TOP, ny)
    inner = (nz + 2 * (DEEP - 1), 2, window, ny)
    field_rows = [message_rows(dx, dz, FIELD_DEPTHS, nz, nx) for dx, dz in WAYS]
    coef_rows = [message_rows(dx, dz, COEF_DEPTHS, nz, nx) for dx, dz in WAYS]
    images, source_out, receiver_out = pl.pallas_call(
        functools.partial(kernel, sizes),
        out_shape=(
            jax.ShapeDtypeStruct((nlag, nz * nx, ny), bf16),
            jax.ShapeDtypeStruct(source_fields.shape, f32),
            jax.ShapeDtypeStruct(receiver_fields.shape, f32),
        ),
        in_specs=[hbm] * 12,
        out_specs=(vmem, vmem, vmem),
        scratch_shapes=[
            pltpu.VMEM((2, *whole), f32),
            pltpu.VMEM((2, *whole), f32),
            pltpu.VMEM((2, *whole), f32),
            pltpu.VMEM((4, *whole), f32),
            pltpu.VMEM((6, *inner), f32),
            pltpu.VMEM((STEPS, *inner), f32),
            pltpu.VMEM((4, nz, nx, ny), f32),
            pltpu.VMEM((4, nz, nx, ny), f32),
            pltpu.VMEM((2, 4, nz, nx, ny), f32),
            *[pltpu.VMEM((SNAPS, 2, count, ny), f32) for count in field_rows * 2],
            *[pltpu.VMEM((2, count, ny), f32) for count in coef_rows * 2],
            pltpu.VMEM((SNAPS, 2, nz * nx, ny), bf16),
            pltpu.VMEM((SNAPS, len(SNAP_WAYS), 2, nz * nx, ny), bf16),
            pltpu.VMEM((SNAPS, 2, nz, 3 * nx, ny), f32),
            pltpu.VMEM((SNAPS, 2, nz, 3 * nx, ny), f32),
            pltpu.VMEM((nlag, nz * nx, ny), f32),
            pltpu.VMEM((2, 4, nz, nx, ny), f32),
            pltpu.VMEM((4, nz, nx, ny), f32),
            pltpu.SemaphoreType.DMA((11,)),
            pltpu.SemaphoreType.DMA((6,)),
            pltpu.SemaphoreType.DMA((6,)),
            pltpu.SemaphoreType.DMA((SNAPS + 1, len(WAYS))),
            pltpu.SemaphoreType.DMA((SNAPS + 1, len(WAYS))),
            pltpu.SemaphoreType.DMA((SNAPS, len(SNAP_WAYS))),
            pltpu.SemaphoreType.DMA((SNAPS, len(SNAP_WAYS))),
            pltpu.SMEM(source_pos.shape, jnp.int32),
            pltpu.SMEM(wavelet.shape, f32),
            pltpu.SMEM(step_counts.shape, jnp.int32),
            pltpu.SMEM(offset_lags.shape[::-1], jnp.int32),
            pltpu.VMEM(receiver_pos.shape[::-1], jnp.int32),
            pltpu.VMEM(receiver_data.shape, f32),
        ],
        compiler_params=pltpu.CompilerParams(
            collective_id=0, has_side_effects=True, vmem_limit_bytes=48 * 1024 * 1024
        ),
    )(
        *(
            pltpu.with_memory_space_constraint(x, pltpu.HBM)
            for x in (
                source_fields,
                receiver_fields,
                courant,
                epsilon,
                delta_param,
                tilt_angle,
                source_pos,
                wavelet,
                receiver_pos.T,
                receiver_data,
                step_counts,
                offset_lags.T,
            )
        )
    )
    return images.reshape(nlag, nz, nx, ny), source_out, receiver_out


def solution(mesh):
    fields = P("shot", "sec", "gx", "gy")
    grid = P("sec", "gx", "gy")
    sizes = tuple(mesh.shape[axis] for axis in ("gx", "sec", "gy"))
    return jax.shard_map(
        functools.partial(local, sizes),
        mesh=mesh,
        in_specs=(
            fields,
            fields,
            grid,
            grid,
            grid,
            grid,
            P("shot"),
            P("shot"),
            P("shot", None),
            P("shot", None),
            P(),
            P(),
        ),
        out_specs=(fields, fields, fields),
        check_vma=False,
    )
```

```python
import functools

import jax
import jax.numpy as jnp
from jax import lax
from jax.experimental import pallas as pl
from jax.experimental.pallas import tpu as pltpu
from jax.sharding import PartitionSpec as P

SNAPS = 3
STEPS = 3
DEEP = STEPS
MESH = pl.DeviceIdType.MESH

TOP = 8
SIDE = 4
WAYS = ((-1, 0), (1, 0), (0, -1), (0, 1), (-1, -1), (-1, 1), (1, -1), (1, 1))
SNAP_WAYS = ((-1, False), (1, False), (0, True), (-1, True), (1, True))


def layers(dx, dz, depth, nz, nx):
    if dz == 0:
        z_from, z_to, z_count = DEEP, DEEP, nz
    elif dz < 0:
        z_from, z_to, z_count = DEEP, DEEP + nz, depth
    else:
        z_from, z_to, z_count = DEEP + nz - depth, DEEP - depth, depth
    first = TOP + SIDE
    if dx == 0:
        x_from, x_to, x_count = first, first, nx
    elif dx < 0:
        x_from, x_to, x_count = first, first + nx, depth
    else:
        x_from, x_to, x_count = first + nx - depth, first - depth, depth
    return z_from, z_to, z_count, x_from, x_to, x_count


def message_rows(dx, dz, depths, nz, nx):
    total = 0
    for depth in depths:
        _, _, z_count, _, _, x_count = layers(dx, dz, depth, nz, nx)
        total += z_count * x_count
    return -(-total // 8) * 8


FIELD_DEPTHS = (DEEP, DEEP, DEEP - 1, DEEP - 1)
COEF_DEPTHS = (DEEP - 1,) * 4


def lag_product(centre, beside, lag_ref, lag):
    nx, ny = centre.shape[2] // 3, centre.shape[3]
    lane = lax.broadcasted_iota(jnp.int32, (nx, ny), 1)
    lx = lag_ref[0, lag]
    ly = lag_ref[1, lag]

    def shifted(h, sx, sy):
        c = centre[h, :, pl.ds(nx + sx, nx), :]
        b = beside[h, :, pl.ds(nx + sx, nx), :]
        edge = jnp.logical_or(lane < sy, lane >= ny + sy)
        mixed = jnp.where(edge[None], b, c)
        return pltpu.roll(mixed, lax.rem(ny - sy, ny), 2)

    product = shifted(0, -lx, -ly) * shifted(1, lx, ly)
    return product.reshape(-1, ny)


def over_lags(first, last, action):
    some = 4 if (last - first) % 4 == 0 else 1

    def lags(i, carry):
        for more in range(some):
            action(first + i * some + more)
        return carry

    lax.fori_loop(0, (last - first) // some, lags, 0)


def finish(
    centre, beside, acc, lag_ref, both, img_out, so_out, ro_out, img, sems
):
    nlag = img.shape[0]
    parts = 4 if nlag % 4 == 0 else 1
    copies = [
        pltpu.make_async_copy(both.at[0], so_out, sems.at[parts]),
        pltpu.make_async_copy(both.at[1], ro_out, sems.at[parts + 1]),
    ]
    for copy in copies:
        copy.start()
    for part in range(parts):
        first, last = part * nlag // parts, (part + 1) * nlag // parts

        def one(lag):
            product = lag_product(centre, beside, lag_ref, lag)
            img[lag] = (acc[lag] + product).astype(jnp.bfloat16)

        over_lags(first, last, one)
        copy = pltpu.make_async_copy(
            img.at[first:last], img_out.at[first:last], sems.at[part]
        )
        copy.start()
        copies.append(copy)
    for copy in copies:
        copy.wait()


def kernel(
    sizes,
    src_ref,
    rec_ref,
    cou_ref,
    eps_ref,
    del_ref,
    tilt_ref,
    spos_ref,
    wav_ref,
    rpos_ref,
    rdat_ref,
    cnt_ref,
    lag_ref,
    last_centre,
    last_beside,
    acc,
    lag_out,
    both,
    *scratch,
):
    small_hbm = (spos_ref, wav_ref, cnt_ref, lag_ref, rpos_ref, rdat_ref)
    small = scratch[-6:]
    spos_ref, wav_ref, cnt_ref, lag_ref, rpos_ref, rdat_ref = small
    scratch = scratch[:-6]
    now, new, old, raw, coef, dep = scratch[:6]
    mine, theirs, halves = scratch[6:9]
    field_send, field_recv = scratch[9:17], scratch[17:25]
    coef_send, coef_recv = scratch[25:33], scratch[33:41]
    snap_send, snap_recv, centre, beside, give = scratch[41:46]
    load_sem, pair_ssem, pair_rsem, halo_ssem, halo_rsem, snap_ssem, snap_rsem = scratch[46:]
    nz, nx, ny = cou_ref.shape
    nlag = lag_ref.shape[1]
    window = nx + 2 * SIDE
    first = TOP + SIDE
    rows = slice(TOP, TOP + window)
    block = slice(first, first + nx)
    ngx, nsec, _ = sizes
    gx, sec, gy = lax.axis_index("gx"), lax.axis_index("sec"), lax.axis_index("gy")
    is_source = gy == 0

    def exists(dx, dz):
        ok = None
        if dx:
            ok = gx > 0 if dx < 0 else gx < ngx - 1
        if dz:
            okz = sec > 0 if dz < 0 else sec < nsec - 1
            ok = okz if ok is None else jnp.logical_and(ok, okz)
        return ok

    def guarded(ok, action):
        if ok is None:
            action()
        else:
            pl.when(ok)(action)

    def device(dx, dz, other):
        where = {}
        if dx:
            where["gx"] = gx + dx
        if dz:
            where["sec"] = sec + dz
        if other:
            where["gy"] = 1 - gy
        return where

    def remote(src, dst, send_sem, recv_sem, where):
        return pltpu.make_async_remote_copy(
            src_ref=src,
            dst_ref=dst,
            send_sem=send_sem,
            recv_sem=recv_sem,
            device_id=where,
            device_id_type=MESH,
        )

    coef_refs = (cou_ref, eps_ref, del_ref, tilt_ref)
    loads = [
        pltpu.make_async_copy(ref, halves.at[0, i], load_sem.at[i])
        for i, ref in enumerate(coef_refs)
    ]
    loads += [
        pltpu.make_async_copy(ref, held, load_sem.at[5 + i])
        for i, (ref, held) in enumerate(zip(small_hbm, small))
    ]
    loads.append(pltpu.make_async_copy(small_hbm[3], lag_out, load_sem.at[11]))
    for copy in loads:
        copy.start()
    load_source = pltpu.make_async_copy(src_ref, mine, load_sem.at[4])
    load_receiver = pltpu.make_async_copy(rec_ref, mine, load_sem.at[4])
    pl.when(is_source)(load_source.start)
    pl.when(jnp.logical_not(is_source))(load_receiver.start)

    barrier = pltpu.get_barrier_semaphore()
    total = jnp.int32(1)
    pl.semaphore_signal(barrier, inc=1, device_id=device(0, 0, True), device_id_type=MESH)
    for dx, dz, other in [(dx, dz, False) for dx, dz in WAYS] + [(-1, 0, True), (1, 0, True)]:
        ok = exists(dx, dz)
        total = total + ok.astype(jnp.int32)

        @pl.when(ok)
        def _():
            pl.semaphore_signal(
                barrier, inc=1, device_id=device(dx, dz, other), device_id_type=MESH
            )

    for ref in (now, old, raw):
        ref[:, :, :, rows, :] = jnp.zeros(ref.shape[:3] + (window, ny), jnp.float32)
    for ref in (centre, beside, last_centre, last_beside):
        ref[...] = jnp.zeros_like(ref)
    pl.semaphore_wait(barrier, total)

    pairs = [
        remote(ref, halves.at[1, i], pair_ssem.at[i], pair_rsem.at[i], device(0, 0, True))
        for i, ref in enumerate(coef_refs)
    ]
    to_pair = device(0, 0, True)
    swap_receiver = remote(rec_ref, theirs, pair_ssem.at[4], pair_rsem.at[4], to_pair)
    swap_source = remote(src_ref, theirs, pair_ssem.at[4], pair_rsem.at[4], to_pair)
    for copy in pairs:
        copy.start()
    pl.when(is_source)(swap_receiver.start)
    pl.when(jnp.logical_not(is_source))(swap_source.start)

    def joined(own, other):
        left = jnp.where(is_source, own, other)
        right = jnp.where(is_source, other, own)
        return left, right

    def split(left, right):
        return jnp.where(is_source, left, right), jnp.where(is_source, right, left)

    def pack(buffer, arrays, depths, dx, dz):
        at = 0
        for (ref, f), depth in zip(arrays, depths):
            z_from, _, z_count, x_from, _, x_count = layers(dx, dz, depth, nz, nx)
            for z in range(z_count):
                buffer[:, at : at + x_count, :] = ref[f, z_from + z, :, x_from : x_from + x_count, :]
                at += x_count

    def unpack(buffer, arrays, depths, dx, dz):
        at = 0
        for (ref, f), depth in zip(arrays, depths):
            _, z_to, z_count, _, x_to, x_count = layers(dx, dz, depth, nz, nx)
            for z in range(z_count):
                ref[f, z_to + z, :, x_to : x_to + x_count, :] = buffer[:, at : at + x_count, :]
                at += x_count

    coef_arrays = [(raw, i) for i in range(4)]
    field_arrays = [(now, 0), (now, 1), (old, 0), (old, 1)]

    def coef_copy(n):
        return remote(
            coef_send[n],
            coef_recv[n],
            halo_ssem.at[SNAPS, n],
            halo_rsem.at[SNAPS, n],
            device(*WAYS[n], False),
        )

    def field_copy(s, n):
        return remote(
            field_send[n].at[s],
            field_recv[n].at[s],
            halo_ssem.at[s, n],
            halo_rsem.at[s, n],
            device(*WAYS[n], False),
        )

    def send_fields(s):
        for n, (dx, dz) in enumerate(WAYS):

            def go():
                pack(field_send[n].at[s], field_arrays, FIELD_DEPTHS, dx, dz)
                field_copy(s, n).start()

            guarded(exists(dx, dz), go)

    def take_fields(s):
        for n, (dx, dz) in enumerate(WAYS):

            def go():
                field_copy(s, n).wait_recv()
                unpack(field_recv[n].at[s], field_arrays, FIELD_DEPTHS, dx, dz)

            guarded(exists(-dx, -dz), go)

    for copy in loads:
        copy.wait()
    load_source.wait()
    for copy in pairs:
        copy.wait_recv()
    swap_source.wait_recv()
    for ref, f, own, other in [
        (raw, i, halves.at[0, i], halves.at[1, i]) for i in range(4)
    ] + [(ref, f, mine.at[i], theirs.at[i]) for i, (ref, f) in enumerate(field_arrays)]:
        left, right = joined(own[...], other[...])
        ref[f, DEEP : DEEP + nz, 0, block, :] = left
        ref[f, DEEP : DEEP + nz, 1, block, :] = right

    for n, (dx, dz) in enumerate(WAYS):

        def go():
            pack(coef_send[n], coef_arrays, COEF_DEPTHS, dx, dz)
            coef_copy(n).start()

        guarded(exists(dx, dz), go)

    planes = nz + 2 * (DEEP - 1)

    def deposits(s):
        nrec = rpos_ref.shape[1]
        lane = lax.broadcasted_iota(jnp.int32, (1, nrec), 1)

        def points(d):
            alone = jnp.where(lane == 0, spos_ref[d], -1)
            return jnp.where(is_source, alone, rpos_ref[d : d + 1, :])

        pz = points(0) - sec * nz + (DEEP - 1)
        px = points(1) - gx * nx + SIDE
        py = points(2)
        at_y = lax.broadcasted_iota(jnp.int32, (2 * ny, nrec), 0) == py
        at_y = jnp.where(at_y, 1.0, 0.0).astype(jnp.bfloat16)
        cell = jnp.where((px >= 0) & (px < window), pz * window + px, -1)
        at_cell = lax.broadcasted_iota(jnp.int32, (planes * window, nrec), 0) == cell
        for j in range(STEPS):
            t = s * STEPS + j
            alone = jnp.where(lane == 0, wav_ref[t], 0.0)
            amounts = jnp.where(is_source, alone, rdat_ref[pl.ds(t, 1), :])
            high = amounts.astype(jnp.bfloat16).astype(jnp.float32)
            summed = None
            for part in (high, amounts - high):
                picked = jnp.where(at_cell, part, 0.0).astype(jnp.bfloat16)
                term = lax.dot_general(
                    picked, at_y, (((1,), (1,)), ((), ())), preferred_element_type=jnp.float32
                )
                summed = term if summed is None else summed + term
            for half in range(2):
                lanes = summed[:, half * ny : (half + 1) * ny]
                dep[j, :, half] = lanes.reshape(planes, window, ny)

    def coefficients():
        for n, (dx, dz) in enumerate(WAYS):

            def go():
                coef_copy(n).wait_recv()
                unpack(coef_recv[n], coef_arrays, COEF_DEPTHS, dx, dz)

            guarded(exists(-dx, -dz), go)

        def plane(z, carry):
            tilt = raw[3, 1 + z, :, rows, :]
            cos_tilt, sin_tilt = jnp.cos(tilt), jnp.sin(tilt)
            coef[0, z] = raw[0, 1 + z, :, rows, :]
            coef[1, z] = 1.0 + 2.0 * raw[1, 1 + z, :, rows, :]
            coef[2, z] = 1.0 + 2.0 * raw[2, 1 + z, :, rows, :]
            coef[3, z] = cos_tilt * cos_tilt
            coef[4, z] = sin_tilt * sin_tilt
            coef[5, z] = 0.5 * sin_tilt * cos_tilt
            return carry

        lax.fori_loop(0, planes, plane, 0)

    def snap_copy(s, n):
        dx, other = SNAP_WAYS[n]
        return remote(
            snap_send.at[s],
            snap_recv.at[s, n],
            snap_ssem.at[s, n],
            snap_rsem.at[s, n],
            device(dx, 0, other),
        )

    lane = lax.broadcasted_iota(jnp.int32, (nx, ny), 1)
    keep = (lane < ny // 2) == is_source

    def pair_of(s):
        if isinstance(s, int) and s == SNAPS - 1:
            return last_centre, last_beside
        return centre.at[s], beside.at[s]

    def place(s, section, dx, whole):
        start = nx - dx * nx
        whole = whole.astype(jnp.float32)
        own, other = split(whole[0].reshape(nz, nx, ny), whole[1].reshape(nz, nx, ny))
        to_centre, to_beside = pair_of(s)
        to_centre[section, :, start : start + nx, :] = own
        to_beside[section, :, start : start + nx, :] = jnp.where(keep[None], other, 0.0)

    def send_snapshot(s, ref):
        for half in range(2):
            rounded = ref[0, DEEP : DEEP + nz, half, block, :].astype(jnp.bfloat16)
            snap_send[s, half] = rounded.reshape(nz * nx, ny)
        for n, (dx, other) in enumerate(SNAP_WAYS):
            guarded(exists(dx, 0), snap_copy(s, n).start)
        place(s, gy, 0, snap_send[s])

    def take_snapshot(s):
        for n, (dx, other) in enumerate(SNAP_WAYS):

            def go():
                snap_copy(s, n).wait_recv()
                place(s, 1 - gy if other else gy, dx, snap_recv[s, n])

            guarded(exists(-dx, 0), go)

    def image(s):
        def one(lag):
            product = lag_product(*pair_of(s), lag_ref, lag)
            if s == 0:
                acc[lag] = product
            else:
                acc[lag] = acc[lag] + product

        over_lags(0, nlag, one)

    def advance(j, halo, active, here, there):
        skip = SIDE if halo == 0 else 0
        start, stop = TOP + skip, TOP + window - skip
        rows = slice(start, stop)
        inner = slice(skip, window - skip)
        step_lane = lax.broadcasted_iota(jnp.int32, (stop - start, ny), 1)
        first_lane = step_lane == 0
        last_lane = step_lane == ny - 1
        for z in range(DEEP - halo, DEEP + nz + halo):
            c = z - 1
            left, right = here[0, z, 0, rows, :], here[0, z, 1, rows, :]
            left_up, right_up = pltpu.roll(left, ny - 1, 1), pltpu.roll(right, ny - 1, 1)
            left_down, right_down = pltpu.roll(left, 1, 1), pltpu.roll(right, 1, 1)
            sides = (
                jnp.where(last_lane, right_up, left_up) + jnp.where(first_lane, 0.0, left_down),
                jnp.where(last_lane, 0.0, right_up) + jnp.where(first_lane, left_down, right_down),
            )
            for half in range(2):

                def diffs(f):
                    def at(dz, dx):
                        return here[f, z + dz, half, start + dx : stop + dx, :]

                    mid = at(0, 0)
                    twice = 2.0 * mid
                    zz = at(1, 0) + at(-1, 0) - twice
                    xx = at(0, 1) + at(0, -1) - twice
                    xz = at(1, 1) - at(1, -1) - at(-1, 1) + at(-1, -1)
                    return mid, twice, zz, xx, xz

                p, twice_p, pzz, pxx, pxz = diffs(0)
                q, twice_q, qzz, qxx, qxz = diffs(1)
                pyy = sides[half] - twice_p
                wz, wx, wm = (coef[i, c, half, inner, :] for i in (3, 4, 5))
                vert_p = wz * pzz + wx * pxx + wm * pxz
                horiz = pzz + pxx + pyy - vert_p
                vert_q = wz * qzz + wx * qxx + wm * qxz
                p_old, q_old = old[0, z, half, rows, :], old[1, z, half, rows, :]
                amount = dep[j, c, half, inner, :]
                cou = coef[0, c, half, inner, :]
                new_p = twice_p - p_old + cou * (coef[1, c, half, inner, :] * horiz + vert_q) + amount
                new_q = twice_q - q_old + cou * (coef[2, c, half, inner, :] * horiz + vert_q) + amount
                there[0, z, half, rows, :] = jnp.where(active, new_p, p)
                there[1, z, half, rows, :] = jnp.where(active, new_q, q)
                old[0, z, half, rows, :] = jnp.where(active, p, p_old)
                old[1, z, half, rows, :] = jnp.where(active, q, q_old)

    def window_steps(s, carry):
        send_fields(s)

        @pl.when(s > 0)
        def _():
            send_snapshot(s - 1, now)

        deposits(s)
        pl.when(s == 0)(coefficients)

        @pl.when(s == SNAPS - 1)
        def _():
            take_snapshot(0)
            image(0)

        take_fields(s)
        here, there = now, new
        for j in range(STEPS):
            advance(j, STEPS - 1 - j, j < cnt_ref[s], here, there)
            here, there = there, here
        if here is new:
            for f in range(2):
                now[f, DEEP : DEEP + nz, :, block, :] = new[f, DEEP : DEEP + nz, :, block, :]
        return carry

    lax.fori_loop(0, SNAPS, window_steps, 0)

    send_snapshot(SNAPS - 1, now)
    for i, (ref, f) in enumerate(field_arrays):
        own, other = split(
            ref[f, DEEP : DEEP + nz, 0, block, :], ref[f, DEEP : DEEP + nz, 1, block, :]
        )
        both[gy, i] = own
        give[i] = other
    back = remote(give, both.at[gy], pair_ssem.at[5], pair_rsem.at[5], to_pair)
    back.start()
    for s in range(1, SNAPS - 1):
        take_snapshot(s)
        image(s)
    take_snapshot(SNAPS - 1)
    remote(give, both.at[1 - gy], pair_ssem.at[5], pair_rsem.at[5], to_pair).wait_recv()

    back.wait_send()
    for copy in pairs:
        copy.wait_send()
    swap_source.wait_send()
    for n, (dx, dz) in enumerate(WAYS):

        def ended():
            coef_copy(n).wait_send()
            for s in range(SNAPS):
                field_copy(s, n).wait_send()

        guarded(exists(dx, dz), ended)
    for n, (dx, _) in enumerate(SNAP_WAYS):

        def ended():
            for s in range(SNAPS):
                snap_copy(s, n).wait_send()

        guarded(exists(dx, 0), ended)


def local(
    sizes,
    source_fields,
    receiver_fields,
    courant,
    epsilon,
    delta_param,
    tilt_angle,
    source_pos,
    wavelet,
    receiver_pos,
    receiver_data,
    step_counts,
    offset_lags,
):
    nz, nx, ny = courant.shape
    nlag = offset_lags.shape[0]
    f32, bf16 = jnp.float32, jnp.bfloat16
    vmem = pl.BlockSpec(memory_space=pltpu.VMEM)
    hbm = pl.BlockSpec(memory_space=pltpu.HBM)
    window = nx + 2 * SIDE
    whole = (nz + 2 * DEEP, 2, window + 2 * TOP, ny)
    inner = (nz + 2 * (DEEP - 1), 2, window, ny)
    field_rows = [message_rows(dx, dz, FIELD_DEPTHS, nz, nx) for dx, dz in WAYS]
    coef_rows = [message_rows(dx, dz, COEF_DEPTHS, nz, nx) for dx, dz in WAYS]
    edged = jax.ShapeDtypeStruct((2, nz, 3 * nx, ny), f32)
    held = pl.pallas_call(
        functools.partial(kernel, sizes),
        out_shape=(
            edged,
            edged,
            jax.ShapeDtypeStruct((nlag, nz * nx, ny), f32),
            jax.ShapeDtypeStruct(offset_lags.shape[::-1], jnp.int32),
            jax.ShapeDtypeStruct((2, 4, nz, nx, ny), f32),
        ),
        in_specs=[hbm] * 12,
        out_specs=(vmem,) * 5,
        scratch_shapes=[
            pltpu.VMEM((2, *whole), f32),
            pltpu.VMEM((2, *whole), f32),
            pltpu.VMEM((2, *whole), f32),
            pltpu.VMEM((4, *whole), f32),
            pltpu.VMEM((6, *inner), f32),
            pltpu.VMEM((STEPS, *inner), f32),
            pltpu.VMEM((4, nz, nx, ny), f32),
            pltpu.VMEM((4, nz, nx, ny), f32),
            pltpu.VMEM((2, 4, nz, nx, ny), f32),
            *[pltpu.VMEM((SNAPS, 2, count, ny), f32) for count in field_rows * 2],
            *[pltpu.VMEM((2, count, ny), f32) for count in coef_rows * 2],
            pltpu.VMEM((SNAPS, 2, nz * nx, ny), bf16),
            pltpu.VMEM((SNAPS, len(SNAP_WAYS), 2, nz * nx, ny), bf16),
            pltpu.VMEM((SNAPS - 1, 2, nz, 3 * nx, ny), f32),
            pltpu.VMEM((SNAPS - 1, 2, nz, 3 * nx, ny), f32),
            pltpu.VMEM((4, nz, nx, ny), f32),
            pltpu.SemaphoreType.DMA((12,)),
            pltpu.SemaphoreType.DMA((6,)),
            pltpu.SemaphoreType.DMA((6,)),
            pltpu.SemaphoreType.DMA((SNAPS + 1, len(WAYS))),
            pltpu.SemaphoreType.DMA((SNAPS + 1, len(WAYS))),
            pltpu.SemaphoreType.DMA((SNAPS, len(SNAP_WAYS))),
            pltpu.SemaphoreType.DMA((SNAPS, len(SNAP_WAYS))),
            pltpu.SMEM(source_pos.shape, jnp.int32),
            pltpu.SMEM(wavelet.shape, f32),
            pltpu.SMEM(step_counts.shape, jnp.int32),
            pltpu.SMEM(offset_lags.shape[::-1], jnp.int32),
            pltpu.VMEM(receiver_pos.shape[::-1], jnp.int32),
            pltpu.VMEM(receiver_data.shape, f32),
        ],
        compiler_params=pltpu.CompilerParams(
            collective_id=0, has_side_effects=True, vmem_limit_bytes=48 * 1024 * 1024
        ),
    )(
        *(
            pltpu.with_memory_space_constraint(x, pltpu.HBM)
            for x in (
                source_fields,
                receiver_fields,
                courant,
                epsilon,
                delta_param,
                tilt_angle,
                source_pos,
                wavelet,
                receiver_pos.T,
                receiver_data,
                step_counts,
                offset_lags.T,
            )
        )
    )
    images, source_out, receiver_out = pl.pallas_call(
        finish,
        out_shape=(
            pltpu.HBM((nlag, nz * nx, ny), bf16),
            pltpu.HBM(source_fields.shape, f32),
            pltpu.HBM(receiver_fields.shape, f32),
        ),
        in_specs=[vmem] * 3 + [pl.BlockSpec(memory_space=pltpu.SMEM), vmem],
        out_specs=(hbm,) * 3,
        scratch_shapes=[
            pltpu.VMEM((nlag, nz * nx, ny), bf16),
            pltpu.SemaphoreType.DMA((6,)),
        ],
    )(*held)
    return images.reshape(nlag, nz, nx, ny), source_out, receiver_out


def solution(mesh):
    fields = P("shot", "sec", "gx", "gy")
    grid = P("sec", "gx", "gy")
    sizes = tuple(mesh.shape[axis] for axis in ("gx", "sec", "gy"))
    return jax.shard_map(
        functools.partial(local, sizes),
        mesh=mesh,
        in_specs=(
            fields,
            fields,
            grid,
            grid,
            grid,
            grid,
            P("shot"),
            P("shot"),
            P("shot", None),
            P("shot", None),
            P(),
            P(),
        ),
        out_specs=(fields, fields, fields),
        check_vma=False,
    )
```

```python
import functools

import jax
import jax.numpy as jnp
from jax import lax
from jax.experimental import pallas as pl
from jax.experimental.pallas import tpu as pltpu
from jax.sharding import PartitionSpec as P

SNAPS = 3
STEPS = 3
DEEP = STEPS
MESH = pl.DeviceIdType.MESH

TOP = 8
SIDE = 4
WAYS = ((-1, 0), (1, 0), (0, -1), (0, 1), (-1, -1), (-1, 1), (1, -1), (1, 1))
SNAP_WAYS = ((-1, False), (1, False), (0, True), (-1, True), (1, True))


def layers(dx, dz, depth, nz, nx):
    if dz == 0:
        z_from, z_to, z_count = DEEP, DEEP, nz
    elif dz < 0:
        z_from, z_to, z_count = DEEP, DEEP + nz, depth
    else:
        z_from, z_to, z_count = DEEP + nz - depth, DEEP - depth, depth
    first = TOP + SIDE
    if dx == 0:
        x_from, x_to, x_count = first, first, nx
    elif dx < 0:
        x_from, x_to, x_count = first, first + nx, depth
    else:
        x_from, x_to, x_count = first + nx - depth, first - depth, depth
    return z_from, z_to, z_count, x_from, x_to, x_count


def message_rows(dx, dz, depths, nz, nx):
    total = 0
    for depth in depths:
        _, _, z_count, _, _, x_count = layers(dx, dz, depth, nz, nx)
        total += z_count * x_count
    return -(-total // 8) * 8


FIELD_DEPTHS = (DEEP, DEEP, DEEP - 1, DEEP - 1)
COEF_DEPTHS = (DEEP - 1,) * 4


def kernel(
    sizes,
    src_ref,
    rec_ref,
    cou_ref,
    eps_ref,
    del_ref,
    tilt_ref,
    spos_ref,
    wav_ref,
    rpos_ref,
    rdat_ref,
    cnt_ref,
    lag_ref,
    img_ref,
    so_ref,
    ro_ref,
    *scratch,
):
    small_hbm = (spos_ref, wav_ref, cnt_ref, lag_ref, rpos_ref, rdat_ref)
    small = scratch[-6:]
    spos_ref, wav_ref, cnt_ref, lag_ref, rpos_ref, rdat_ref = small
    scratch = scratch[:-6]
    now, new, old, raw, coef, dep = scratch[:6]
    mine, theirs, halves = scratch[6:9]
    field_send, field_recv = scratch[9:17], scratch[17:25]
    coef_send, coef_recv = scratch[25:33], scratch[33:41]
    snap_send, snap_recv, centre, beside, acc, both, give = scratch[41:48]
    load_sem, pair_ssem, pair_rsem, halo_ssem, halo_rsem, snap_ssem, snap_rsem = scratch[48:]
    nz, nx, ny = cou_ref.shape
    nlag = lag_ref.shape[1]
    window = nx + 2 * SIDE
    first = TOP + SIDE
    rows = slice(TOP, TOP + window)
    block = slice(first, first + nx)
    ngx, nsec, _ = sizes
    gx, sec, gy = lax.axis_index("gx"), lax.axis_index("sec"), lax.axis_index("gy")
    is_source = gy == 0

    def exists(dx, dz):
        ok = None
        if dx:
            ok = gx > 0 if dx < 0 else gx < ngx - 1
        if dz:
            okz = sec > 0 if dz < 0 else sec < nsec - 1
            ok = okz if ok is None else jnp.logical_and(ok, okz)
        return ok

    def guarded(ok, action):
        if ok is None:
            action()
        else:
            pl.when(ok)(action)

    def device(dx, dz, other):
        where = {}
        if dx:
            where["gx"] = gx + dx
        if dz:
            where["sec"] = sec + dz
        if other:
            where["gy"] = 1 - gy
        return where

    def remote(src, dst, send_sem, recv_sem, where):
        return pltpu.make_async_remote_copy(
            src_ref=src,
            dst_ref=dst,
            send_sem=send_sem,
            recv_sem=recv_sem,
            device_id=where,
            device_id_type=MESH,
        )

    coef_refs = (cou_ref, eps_ref, del_ref, tilt_ref)
    loads = [
        pltpu.make_async_copy(ref, halves.at[0, i], load_sem.at[i])
        for i, ref in enumerate(coef_refs)
    ]
    loads += [
        pltpu.make_async_copy(ref, held, load_sem.at[5 + i])
        for i, (ref, held) in enumerate(zip(small_hbm, small))
    ]
    for copy in loads:
        copy.start()
    load_source = pltpu.make_async_copy(src_ref, mine, load_sem.at[4])
    load_receiver = pltpu.make_async_copy(rec_ref, mine, load_sem.at[4])
    pl.when(is_source)(load_source.start)
    pl.when(jnp.logical_not(is_source))(load_receiver.start)

    barrier = pltpu.get_barrier_semaphore()
    total = jnp.int32(1)
    pl.semaphore_signal(barrier, inc=1, device_id=device(0, 0, True), device_id_type=MESH)
    for dx, dz, other in [(dx, dz, False) for dx, dz in WAYS] + [(-1, 0, True), (1, 0, True)]:
        ok = exists(dx, dz)
        total = total + ok.astype(jnp.int32)

        @pl.when(ok)
        def _():
            pl.semaphore_signal(
                barrier, inc=1, device_id=device(dx, dz, other), device_id_type=MESH
            )

    for ref in (now, old, raw):
        ref[:, :, :, rows, :] = jnp.zeros(ref.shape[:3] + (window, ny), jnp.float32)
    centre[...] = jnp.zeros_like(centre)
    beside[...] = jnp.zeros_like(beside)
    pl.semaphore_wait(barrier, total)

    pairs = [
        remote(ref, halves.at[1, i], pair_ssem.at[i], pair_rsem.at[i], device(0, 0, True))
        for i, ref in enumerate(coef_refs)
    ]
    to_pair = device(0, 0, True)
    swap_receiver = remote(rec_ref, theirs, pair_ssem.at[4], pair_rsem.at[4], to_pair)
    swap_source = remote(src_ref, theirs, pair_ssem.at[4], pair_rsem.at[4], to_pair)
    for copy in pairs:
        copy.start()
    pl.when(is_source)(swap_receiver.start)
    pl.when(jnp.logical_not(is_source))(swap_source.start)

    def joined(own, other):
        left = jnp.where(is_source, own, other)
        right = jnp.where(is_source, other, own)
        return left, right

    def split(left, right):
        return jnp.where(is_source, left, right), jnp.where(is_source, right, left)

    def pack(buffer, arrays, depths, dx, dz):
        at = 0
        for (ref, f), depth in zip(arrays, depths):
            z_from, _, z_count, x_from, _, x_count = layers(dx, dz, depth, nz, nx)
            chunks = [
                ref[f, z_from + z, :, x_from : x_from + x_count, :] for z in range(z_count)
            ]
            for chunk in chunks:
                buffer[:, at : at + x_count, :] = chunk
                at += x_count

    def unpack(buffer, arrays, depths, dx, dz):
        at = 0
        for (ref, f), depth in zip(arrays, depths):
            _, z_to, z_count, _, x_to, x_count = layers(dx, dz, depth, nz, nx)
            chunks = []
            for z in range(z_count):
                chunks.append(buffer[:, at : at + x_count, :])
                at += x_count
            for z, chunk in enumerate(chunks):
                ref[f, z_to + z, :, x_to : x_to + x_count, :] = chunk

    coef_arrays = [(raw, i) for i in range(4)]
    field_arrays = [(now, 0), (now, 1), (old, 0), (old, 1)]

    def coef_copy(n):
        return remote(
            coef_send[n],
            coef_recv[n],
            halo_ssem.at[SNAPS, n],
            halo_rsem.at[SNAPS, n],
            device(*WAYS[n], False),
        )

    def field_copy(s, n):
        return remote(
            field_send[n].at[s],
            field_recv[n].at[s],
            halo_ssem.at[s, n],
            halo_rsem.at[s, n],
            device(*WAYS[n], False),
        )

    def send_fields(s):
        for n, (dx, dz) in enumerate(WAYS):

            def go():
                pack(field_send[n].at[s], field_arrays, FIELD_DEPTHS, dx, dz)
                field_copy(s, n).start()

            guarded(exists(dx, dz), go)

    def take_fields(s):
        for n, (dx, dz) in enumerate(WAYS):

            def go():
                field_copy(s, n).wait_recv()
                unpack(field_recv[n].at[s], field_arrays, FIELD_DEPTHS, dx, dz)

            guarded(exists(-dx, -dz), go)

    for copy in loads:
        copy.wait()
    load_source.wait()
    for copy in pairs:
        copy.wait_recv()
    swap_source.wait_recv()
    for ref, f, own, other in [
        (raw, i, halves.at[0, i], halves.at[1, i]) for i in range(4)
    ] + [(ref, f, mine.at[i], theirs.at[i]) for i, (ref, f) in enumerate(field_arrays)]:
        left, right = joined(own[...], other[...])
        ref[f, DEEP : DEEP + nz, 0, block, :] = left
        ref[f, DEEP : DEEP + nz, 1, block, :] = right

    for n, (dx, dz) in enumerate(WAYS):

        def go():
            pack(coef_send[n], coef_arrays, COEF_DEPTHS, dx, dz)
            coef_copy(n).start()

        guarded(exists(dx, dz), go)

    planes = nz + 2 * (DEEP - 1)

    def deposits(s):
        nrec = rpos_ref.shape[1]
        lane = lax.broadcasted_iota(jnp.int32, (1, nrec), 1)

        def points(d):
            alone = jnp.where(lane == 0, spos_ref[d], -1)
            return jnp.where(is_source, alone, rpos_ref[d : d + 1, :])

        pz = points(0) - sec * nz + (DEEP - 1)
        px = points(1) - gx * nx + SIDE
        py = points(2)
        at_y = lax.broadcasted_iota(jnp.int32, (2 * ny, nrec), 0) == py
        at_y = jnp.where(at_y, 1.0, 0.0).astype(jnp.bfloat16)
        cell = jnp.where((px >= 0) & (px < window), pz * window + px, -1)
        at_cell = lax.broadcasted_iota(jnp.int32, (planes * window, nrec), 0) == cell
        for j in range(STEPS):
            t = s * STEPS + j
            alone = jnp.where(lane == 0, wav_ref[t], 0.0)
            amounts = jnp.where(is_source, alone, rdat_ref[pl.ds(t, 1), :])
            high = amounts.astype(jnp.bfloat16).astype(jnp.float32)
            summed = None
            for part in (high, amounts - high):
                picked = jnp.where(at_cell, part, 0.0).astype(jnp.bfloat16)
                term = lax.dot_general(
                    picked, at_y, (((1,), (1,)), ((), ())), preferred_element_type=jnp.float32
                )
                summed = term if summed is None else summed + term
            for half in range(2):
                lanes = summed[:, half * ny : (half + 1) * ny]
                dep[j, :, half] = lanes.reshape(planes, window, ny)

    def coefficients():
        for n, (dx, dz) in enumerate(WAYS):

            def go():
                coef_copy(n).wait_recv()
                unpack(coef_recv[n], coef_arrays, COEF_DEPTHS, dx, dz)

            guarded(exists(-dx, -dz), go)

        def plane(z, carry):
            tilt = raw[3, 1 + z, :, rows, :]
            cos_tilt, sin_tilt = jnp.cos(tilt), jnp.sin(tilt)
            coef[0, z] = raw[0, 1 + z, :, rows, :]
            coef[1, z] = 1.0 + 2.0 * raw[1, 1 + z, :, rows, :]
            coef[2, z] = 1.0 + 2.0 * raw[2, 1 + z, :, rows, :]
            coef[3, z] = cos_tilt * cos_tilt
            coef[4, z] = sin_tilt * sin_tilt
            coef[5, z] = 0.5 * sin_tilt * cos_tilt
            return carry

        lax.fori_loop(0, planes, plane, 0)

    def snap_copy(s, n):
        dx, other = SNAP_WAYS[n]
        return remote(
            snap_send.at[s],
            snap_recv.at[s, n],
            snap_ssem.at[s, n],
            snap_rsem.at[s, n],
            device(dx, 0, other),
        )

    lane = lax.broadcasted_iota(jnp.int32, (nx, ny), 1)
    keep = (lane < ny // 2) == is_source

    def place(s, section, dx, whole):
        start = nx - dx * nx
        whole = whole.astype(jnp.float32)
        own, other = split(whole[0].reshape(nz, nx, ny), whole[1].reshape(nz, nx, ny))
        centre[s, section, :, start : start + nx, :] = own
        beside[s, section, :, start : start + nx, :] = jnp.where(keep[None], other, 0.0)

    def send_snapshot(s, ref):
        for half in range(2):
            rounded = ref[0, DEEP : DEEP + nz, half, block, :].astype(jnp.bfloat16)
            snap_send[s, half] = rounded.reshape(nz * nx, ny)
        for n, (dx, other) in enumerate(SNAP_WAYS):
            guarded(exists(dx, 0), snap_copy(s, n).start)
        place(s, gy, 0, snap_send[s])

    def take_snapshot(s):
        for n, (dx, other) in enumerate(SNAP_WAYS):

            def go():
                snap_copy(s, n).wait_recv()
                place(s, 1 - gy if other else gy, dx, snap_recv[s, n])

            guarded(exists(-dx, 0), go)

    def image(s):
        some = 4 if nlag % 4 == 0 else 1

        def product(lag):
            lx = lag_ref[0, lag]
            ly = lag_ref[1, lag]

            def shifted(h, sx, sy):
                c = centre[s, h, :, pl.ds(nx + sx, nx), :]
                b = beside[s, h, :, pl.ds(nx + sx, nx), :]
                edge = jnp.logical_or(lane < sy, lane >= ny + sy)
                mixed = jnp.where(edge[None], b, c)
                return pltpu.roll(mixed, lax.rem(ny - sy, ny), 2)

            term = shifted(0, -lx, -ly) * shifted(1, lx, ly)
            term = term.reshape(nz * nx, ny)
            return term if s == 0 else acc[lag] + term

        def lags(i, carry):
            terms = [product(i * some + more) for more in range(some)]
            for more, term in enumerate(terms):
                if s < SNAPS - 1:
                    acc[i * some + more] = term
                else:
                    img_ref[i * some + more] = term.astype(jnp.bfloat16)
            return carry

        lax.fori_loop(0, nlag // some, lags, 0)

    def advance(j, halo, active, here, there):
        skip = SIDE if halo == 0 else 0
        start, stop = TOP + skip, TOP + window - skip
        rows = slice(start, stop)
        inner = slice(skip, window - skip)
        step_lane = lax.broadcasted_iota(jnp.int32, (stop - start, ny), 1)
        first_lane = step_lane == 0
        last_lane = step_lane == ny - 1
        for z in range(DEEP - halo, DEEP + nz + halo):
            c = z - 1
            left, right = here[0, z, 0, rows, :], here[0, z, 1, rows, :]
            left_up, right_up = pltpu.roll(left, ny - 1, 1), pltpu.roll(right, ny - 1, 1)
            left_down, right_down = pltpu.roll(left, 1, 1), pltpu.roll(right, 1, 1)
            sides = (
                jnp.where(last_lane, right_up, left_up) + jnp.where(first_lane, 0.0, left_down),
                jnp.where(last_lane, 0.0, right_up) + jnp.where(first_lane, left_down, right_down),
            )
            for half in range(2):

                def diffs(f):
                    def at(dz, dx):
                        return here[f, z + dz, half, start + dx : stop + dx, :]

                    mid = at(0, 0)
                    twice = 2.0 * mid
                    zz = at(1, 0) + at(-1, 0) - twice
                    xx = at(0, 1) + at(0, -1) - twice
                    xz = at(1, 1) - at(1, -1) - at(-1, 1) + at(-1, -1)
                    return mid, twice, zz, xx, xz

                p, twice_p, pzz, pxx, pxz = diffs(0)
                q, twice_q, qzz, qxx, qxz = diffs(1)
                pyy = sides[half] - twice_p
                wz, wx, wm = (coef[i, c, half, inner, :] for i in (3, 4, 5))
                vert_p = wz * pzz + wx * pxx + wm * pxz
                horiz = pzz + pxx + pyy - vert_p
                vert_q = wz * qzz + wx * qxx + wm * qxz
                p_old, q_old = old[0, z, half, rows, :], old[1, z, half, rows, :]
                amount = dep[j, c, half, inner, :]
                cou = coef[0, c, half, inner, :]
                new_p = twice_p - p_old + cou * (coef[1, c, half, inner, :] * horiz + vert_q) + amount
                new_q = twice_q - q_old + cou * (coef[2, c, half, inner, :] * horiz + vert_q) + amount
                there[0, z, half, rows, :] = jnp.where(active, new_p, p)
                there[1, z, half, rows, :] = jnp.where(active, new_q, q)
                old[0, z, half, rows, :] = jnp.where(active, p, p_old)
                old[1, z, half, rows, :] = jnp.where(active, q, q_old)

    def window_steps(s, carry):
        send_fields(s)

        @pl.when(s > 0)
        def _():
            send_snapshot(s - 1, now)

        deposits(s)
        pl.when(s == 0)(coefficients)

        @pl.when(s == SNAPS - 1)
        def _():
            take_snapshot(0)
            image(0)

        take_fields(s)
        here, there = now, new
        for j in range(STEPS):
            advance(j, STEPS - 1 - j, j < cnt_ref[s], here, there)
            here, there = there, here
        if here is new:
            for f in range(2):
                now[f, DEEP : DEEP + nz, :, block, :] = new[f, DEEP : DEEP + nz, :, block, :]
        return carry

    lax.fori_loop(0, SNAPS, window_steps, 0)

    send_snapshot(SNAPS - 1, now)
    for i, (ref, f) in enumerate(field_arrays):
        own, other = split(
            ref[f, DEEP : DEEP + nz, 0, block, :], ref[f, DEEP : DEEP + nz, 1, block, :]
        )
        both[gy, i] = own
        give[i] = other
    back = remote(give, both.at[gy], pair_ssem.at[5], pair_rsem.at[5], to_pair)
    back.start()
    for s in range(1, SNAPS - 1):
        take_snapshot(s)
        image(s)
    take_snapshot(SNAPS - 1)
    image(SNAPS - 1)
    remote(give, both.at[1 - gy], pair_ssem.at[5], pair_rsem.at[5], to_pair).wait_recv()
    so_ref[...] = both[0]
    ro_ref[...] = both[1]

    back.wait_send()
    for copy in pairs:
        copy.wait_send()
    swap_source.wait_send()
    for n, (dx, dz) in enumerate(WAYS):

        def ended():
            coef_copy(n).wait_send()
            for s in range(SNAPS):
                field_copy(s, n).wait_send()

        guarded(exists(dx, dz), ended)
    for n, (dx, _) in enumerate(SNAP_WAYS):

        def ended():
            for s in range(SNAPS):
                snap_copy(s, n).wait_send()

        guarded(exists(dx, 0), ended)


def local(
    sizes,
    source_fields,
    receiver_fields,
    courant,
    epsilon,
    delta_param,
    tilt_angle,
    source_pos,
    wavelet,
    receiver_pos,
    receiver_data,
    step_counts,
    offset_lags,
):
    nz, nx, ny = courant.shape
    nlag = offset_lags.shape[0]
    f32, bf16 = jnp.float32, jnp.bfloat16
    vmem = pl.BlockSpec(memory_space=pltpu.VMEM)
    hbm = pl.BlockSpec(memory_space=pltpu.HBM)
    window = nx + 2 * SIDE
    whole = (nz + 2 * DEEP, 2, window + 2 * TOP, ny)
    inner = (nz + 2 * (DEEP - 1), 2, window, ny)
    field_rows = [message_rows(dx, dz, FIELD_DEPTHS, nz, nx) for dx, dz in WAYS]
    coef_rows = [message_rows(dx, dz, COEF_DEPTHS, nz, nx) for dx, dz in WAYS]
    images, source_out, receiver_out = pl.pallas_call(
        functools.partial(kernel, sizes),
        out_shape=(
            jax.ShapeDtypeStruct((nlag, nz * nx, ny), bf16),
            jax.ShapeDtypeStruct(source_fields.shape, f32),
            jax.ShapeDtypeStruct(receiver_fields.shape, f32),
        ),
        in_specs=[hbm] * 12,
        out_specs=(vmem, vmem, vmem),
        scratch_shapes=[
            pltpu.VMEM((2, *whole), f32),
            pltpu.VMEM((2, *whole), f32),
            pltpu.VMEM((2, *whole), f32),
            pltpu.VMEM((4, *whole), f32),
            pltpu.VMEM((6, *inner), f32),
            pltpu.VMEM((STEPS, *inner), f32),
            pltpu.VMEM((4, nz, nx, ny), f32),
            pltpu.VMEM((4, nz, nx, ny), f32),
            pltpu.VMEM((2, 4, nz, nx, ny), f32),
            *[pltpu.VMEM((SNAPS, 2, count, ny), f32) for count in field_rows * 2],
            *[pltpu.VMEM((2, count, ny), f32) for count in coef_rows * 2],
            pltpu.VMEM((SNAPS, 2, nz * nx, ny), bf16),
            pltpu.VMEM((SNAPS, len(SNAP_WAYS), 2, nz * nx, ny), bf16),
            pltpu.VMEM((SNAPS, 2, nz, 3 * nx, ny), f32),
            pltpu.VMEM((SNAPS, 2, nz, 3 * nx, ny), f32),
            pltpu.VMEM((nlag, nz * nx, ny), f32),
            pltpu.VMEM((2, 4, nz, nx, ny), f32),
            pltpu.VMEM((4, nz, nx, ny), f32),
            pltpu.SemaphoreType.DMA((11,)),
            pltpu.SemaphoreType.DMA((6,)),
            pltpu.SemaphoreType.DMA((6,)),
            pltpu.SemaphoreType.DMA((SNAPS + 1, len(WAYS))),
            pltpu.SemaphoreType.DMA((SNAPS + 1, len(WAYS))),
            pltpu.SemaphoreType.DMA((SNAPS, len(SNAP_WAYS))),
            pltpu.SemaphoreType.DMA((SNAPS, len(SNAP_WAYS))),
            pltpu.SMEM(source_pos.shape, jnp.int32),
            pltpu.SMEM(wavelet.shape, f32),
            pltpu.SMEM(step_counts.shape, jnp.int32),
            pltpu.SMEM(offset_lags.shape[::-1], jnp.int32),
            pltpu.VMEM(receiver_pos.shape[::-1], jnp.int32),
            pltpu.VMEM(receiver_data.shape, f32),
        ],
        compiler_params=pltpu.CompilerParams(
            collective_id=0, has_side_effects=True, vmem_limit_bytes=48 * 1024 * 1024
        ),
    )(
        *(
            pltpu.with_memory_space_constraint(x, pltpu.HBM)
            for x in (
                source_fields,
                receiver_fields,
                courant,
                epsilon,
                delta_param,
                tilt_angle,
                source_pos,
                wavelet,
                receiver_pos.T,
                receiver_data,
                step_counts,
                offset_lags.T,
            )
        )
    )
    return images.reshape(nlag, nz, nx, ny), source_out, receiver_out


def solution(mesh):
    fields = P("shot", "sec", "gx", "gy")
    grid = P("sec", "gx", "gy")
    sizes = tuple(mesh.shape[axis] for axis in ("gx", "sec", "gy"))
    return jax.shard_map(
        functools.partial(local, sizes),
        mesh=mesh,
        in_specs=(
            fields,
            fields,
            grid,
            grid,
            grid,
            grid,
            P("shot"),
            P("shot"),
            P("shot", None),
            P("shot", None),
            P(),
            P(),
        ),
        out_specs=(fields, fields, fields),
        check_vma=False,
    )
```

```python
import functools

import jax
import jax.numpy as jnp
from jax import lax
from jax.experimental import pallas as pl
from jax.experimental.pallas import tpu as pltpu
from jax.sharding import PartitionSpec as P

SNAPS = 3
STEPS = 3
DEEP = STEPS
MESH = pl.DeviceIdType.MESH

TOP = 8
SIDE = 4
WAYS = ((-1, 0), (1, 0), (0, -1), (0, 1), (-1, -1), (-1, 1), (1, -1), (1, 1))
SNAP_WAYS = ((-1, False), (1, False), (0, True), (-1, True), (1, True))


def layers(dx, dz, depth, nz, nx):
    if dz == 0:
        z_from, z_to, z_count = DEEP, DEEP, nz
    elif dz < 0:
        z_from, z_to, z_count = DEEP, DEEP + nz, depth
    else:
        z_from, z_to, z_count = DEEP + nz - depth, DEEP - depth, depth
    first = TOP + SIDE
    if dx == 0:
        x_from, x_to, x_count = first, first, nx
    elif dx < 0:
        x_from, x_to, x_count = first, first + nx, depth
    else:
        x_from, x_to, x_count = first + nx - depth, first - depth, depth
    return z_from, z_to, z_count, x_from, x_to, x_count


def message_rows(dx, dz, depths, nz, nx):
    total = 0
    for depth in depths:
        _, _, z_count, _, _, x_count = layers(dx, dz, depth, nz, nx)
        total += z_count * x_count
    return -(-total // 8) * 8


FIELD_DEPTHS = (DEEP, DEEP, DEEP - 1, DEEP - 1)
COEF_DEPTHS = (DEEP - 1,) * 4


def kernel(
    sizes,
    src_ref,
    rec_ref,
    cou_ref,
    eps_ref,
    del_ref,
    tilt_ref,
    spos_ref,
    wav_ref,
    rpos_ref,
    rdat_ref,
    cnt_ref,
    lag_ref,
    img_ref,
    so_ref,
    ro_ref,
    *scratch,
):
    small_hbm = (spos_ref, wav_ref, cnt_ref, lag_ref, rpos_ref, rdat_ref)
    small = scratch[-6:]
    spos_ref, wav_ref, cnt_ref, lag_ref, rpos_ref, rdat_ref = small
    scratch = scratch[:-6]
    now, new, old, raw, coef, dep = scratch[:6]
    loaded, theirs, coef_own = scratch[6:9]
    field_send, field_recv = scratch[9:17], scratch[17:25]
    coef_send, coef_recv = scratch[25:33], scratch[33:41]
    snap_send, snap_recv, centre, beside, acc, both, give = scratch[41:48]
    load_sem, pair_ssem, pair_rsem, halo_ssem, halo_rsem, snap_ssem, snap_rsem = scratch[48:55]
    first_ssem, first_rsem, *first_send = scratch[55:]
    nz, nx, ny = cou_ref.shape
    nlag = lag_ref.shape[1]
    window = nx + 2 * SIDE
    first = TOP + SIDE
    rows = slice(TOP, TOP + window)
    block = slice(first, first + nx)
    ngx, nsec, _ = sizes
    gx, sec, gy = lax.axis_index("gx"), lax.axis_index("sec"), lax.axis_index("gy")
    is_source = gy == 0

    def exists(dx, dz):
        ok = None
        if dx:
            ok = gx > 0 if dx < 0 else gx < ngx - 1
        if dz:
            okz = sec > 0 if dz < 0 else sec < nsec - 1
            ok = okz if ok is None else jnp.logical_and(ok, okz)
        return ok

    def guarded(ok, action):
        if ok is None:
            action()
        else:
            pl.when(ok)(action)

    def device(dx, dz, other):
        where = {}
        if dx:
            where["gx"] = gx + dx
        if dz:
            where["sec"] = sec + dz
        if other:
            where["gy"] = 1 - gy
        return where

    def remote(src, dst, send_sem, recv_sem, where):
        return pltpu.make_async_remote_copy(
            src_ref=src,
            dst_ref=dst,
            send_sem=send_sem,
            recv_sem=recv_sem,
            device_id=where,
            device_id_type=MESH,
        )

    coef_refs = (cou_ref, eps_ref, del_ref, tilt_ref)
    loads = [
        pltpu.make_async_copy(ref, coef_own.at[i], load_sem.at[i])
        for i, ref in enumerate(coef_refs)
    ]
    loads += [
        pltpu.make_async_copy(ref, held, load_sem.at[5 + i])
        for i, (ref, held) in enumerate(zip(small_hbm, small))
    ]
    loads += [
        pltpu.make_async_copy(src_ref, loaded.at[0], load_sem.at[4]),
        pltpu.make_async_copy(rec_ref, loaded.at[1], load_sem.at[11]),
    ]
    for copy in loads:
        copy.start()

    barrier = pltpu.get_barrier_semaphore()
    total = jnp.int32(1)
    to_pair = device(0, 0, True)
    pl.semaphore_signal(barrier, inc=1, device_id=to_pair, device_id_type=MESH)
    for dx, dz in WAYS:
        ok = exists(dx, dz)
        total = total + 2 * ok.astype(jnp.int32)

        @pl.when(ok)
        def _():
            for other in (False, True):
                pl.semaphore_signal(
                    barrier, inc=1, device_id=device(dx, dz, other), device_id_type=MESH
                )

    for ref in (now, old):
        ref[:, :, :, rows, :] = jnp.zeros(ref.shape[:3] + (window, ny), jnp.float32)
    raw[:, :, gy, rows, :] = jnp.zeros(raw.shape[:2] + (window, ny), jnp.float32)
    centre[...] = jnp.zeros_like(centre)
    beside[...] = jnp.zeros_like(beside)
    pl.semaphore_wait(barrier, total)

    swap_receiver = remote(rec_ref, theirs, pair_ssem.at[0], pair_rsem.at[0], to_pair)
    swap_source = remote(src_ref, theirs, pair_ssem.at[0], pair_rsem.at[0], to_pair)
    pl.when(is_source)(swap_receiver.start)
    pl.when(jnp.logical_not(is_source))(swap_source.start)

    def joined(own, other):
        left = jnp.where(is_source, own, other)
        right = jnp.where(is_source, other, own)
        return left, right

    def split(left, right):
        return jnp.where(is_source, left, right), jnp.where(is_source, right, left)

    def pack(buffer, arrays, depths, dx, dz):
        at = 0
        for (ref, f), depth in zip(arrays, depths):
            z_from, _, z_count, x_from, _, x_count = layers(dx, dz, depth, nz, nx)
            chunks = [
                ref[f, z_from + z, :, x_from : x_from + x_count, :] for z in range(z_count)
            ]
            for chunk in chunks:
                buffer[:, at : at + x_count, :] = chunk
                at += x_count

    def unpack(buffer, arrays, depths, dx, dz):
        at = 0
        for (ref, f), depth in zip(arrays, depths):
            _, z_to, z_count, _, x_to, x_count = layers(dx, dz, depth, nz, nx)
            chunks = []
            for z in range(z_count):
                chunks.append(buffer[:, at : at + x_count, :])
                at += x_count
            for z, chunk in enumerate(chunks):
                ref[f, z_to + z, :, x_to : x_to + x_count, :] = chunk

    field_arrays = [(now, 0), (now, 1), (old, 0), (old, 1)]

    def pack_block(buffer, blocks, depths, dx, dz):
        at = 0
        for block_ref, depth in zip(blocks, depths):
            z_from, _, z_count, x_from, _, x_count = layers(dx, dz, depth, nz, nx)
            z_from, x_from = z_from - DEEP, x_from - first
            chunks = [block_ref[z_from + z, x_from : x_from + x_count, :] for z in range(z_count)]
            for chunk in chunks:
                buffer[at : at + x_count, :] = chunk
                at += x_count

    def coef_copy(n):
        return remote(
            coef_send[n],
            coef_recv[n],
            halo_ssem.at[SNAPS, n],
            halo_rsem.at[SNAPS, n],
            device(*WAYS[n], False),
        )

    def first_copy(n, section):
        where = device(*WAYS[n], False)
        where["gy"] = section
        return remote(
            first_send[n].at[section],
            field_recv[n].at[0, gy],
            first_ssem.at[n, section],
            first_rsem.at[n, gy],
            where,
        )

    def field_copy(s, n):
        return remote(
            field_send[n].at[s],
            field_recv[n].at[s],
            halo_ssem.at[s, n],
            halo_rsem.at[s, n],
            device(*WAYS[n], False),
        )

    def send_fields(s):
        for n, (dx, dz) in enumerate(WAYS):

            def go():
                pack(field_send[n].at[s], field_arrays, FIELD_DEPTHS, dx, dz)
                field_copy(s, n).start()

            guarded(exists(dx, dz), go)

    def take_fields(s):
        for n, (dx, dz) in enumerate(WAYS):

            def go():
                @pl.when(s == 0)
                def _():
                    for half in range(2):
                        remote(
                            first_send[n].at[half],
                            field_recv[n].at[0, half],
                            first_ssem.at[n, half],
                            first_rsem.at[n, half],
                            to_pair,
                        ).wait_recv()

                pl.when(s > 0)(field_copy(s, n).wait_recv)
                unpack(field_recv[n].at[s], field_arrays, FIELD_DEPTHS, dx, dz)

            guarded(exists(-dx, -dz), go)

    for copy in loads:
        copy.wait()
    for n, (dx, dz) in enumerate(WAYS):

        def go():
            pack_block(
                coef_send[n], [coef_own.at[i] for i in range(4)], COEF_DEPTHS, dx, dz
            )
            coef_copy(n).start()

        guarded(exists(dx, dz), go)
    for n, (dx, dz) in enumerate(WAYS):

        def go():
            for section in range(2):
                blocks = [loaded.at[section, f] for f in range(4)]
                pack_block(first_send[n].at[section], blocks, FIELD_DEPTHS, dx, dz)
                first_copy(n, section).start()

        guarded(exists(dx, dz), go)
    for i in range(4):
        raw[i, DEEP : DEEP + nz, gy, block, :] = coef_own[i]

    planes = nz + 2 * (DEEP - 1)

    def deposits(s):
        nrec = rpos_ref.shape[1]
        lane = lax.broadcasted_iota(jnp.int32, (1, nrec), 1)

        def points(d):
            alone = jnp.where(lane == 0, spos_ref[d], -1)
            return jnp.where(is_source, alone, rpos_ref[d : d + 1, :])

        pz = points(0) - sec * nz + (DEEP - 1)
        px = points(1) - gx * nx + SIDE
        py = points(2)
        at_y = lax.broadcasted_iota(jnp.int32, (2 * ny, nrec), 0) == py
        at_y = jnp.where(at_y, 1.0, 0.0).astype(jnp.bfloat16)
        cell = jnp.where((px >= 0) & (px < window), pz * window + px, -1)
        at_cell = lax.broadcasted_iota(jnp.int32, (planes * window, nrec), 0) == cell
        for j in range(STEPS):
            t = s * STEPS + j
            alone = jnp.where(lane == 0, wav_ref[t], 0.0)
            amounts = jnp.where(is_source, alone, rdat_ref[pl.ds(t, 1), :])
            high = amounts.astype(jnp.bfloat16).astype(jnp.float32)
            summed = None
            for part in (high, amounts - high):
                picked = jnp.where(at_cell, part, 0.0).astype(jnp.bfloat16)
                term = lax.dot_general(
                    picked, at_y, (((1,), (1,)), ((), ())), preferred_element_type=jnp.float32
                )
                summed = term if summed is None else summed + term
            for half in range(2):
                lanes = summed[:, half * ny : (half + 1) * ny]
                dep[j, :, half] = lanes.reshape(planes, window, ny)

    def share(half):
        part = raw.at[:, 1 : 1 + planes, half, rows, :]
        return remote(part, part, pair_ssem.at[1], pair_rsem.at[1], to_pair)

    def take_coefficients():
        for n, (dx, dz) in enumerate(WAYS):

            def go():
                coef_copy(n).wait_recv()
                at = 0
                for i, depth in enumerate(COEF_DEPTHS):
                    _, z_to, z_count, _, x_to, x_count = layers(dx, dz, depth, nz, nx)
                    chunks = []
                    for z in range(z_count):
                        chunks.append(coef_recv[n][at : at + x_count, :])
                        at += x_count
                    for z, chunk in enumerate(chunks):
                        raw[i, z_to + z, gy, x_to : x_to + x_count, :] = chunk

            guarded(exists(-dx, -dz), go)
        share(gy).start()

    def coefficients():
        share(1 - gy).wait_recv()

        def plane(z, carry):
            tilt = raw[3, 1 + z, :, rows, :]
            cos_tilt, sin_tilt = jnp.cos(tilt), jnp.sin(tilt)
            coef[0, z] = raw[0, 1 + z, :, rows, :]
            coef[1, z] = 1.0 + 2.0 * raw[1, 1 + z, :, rows, :]
            coef[2, z] = 1.0 + 2.0 * raw[2, 1 + z, :, rows, :]
            coef[3, z] = cos_tilt * cos_tilt
            coef[4, z] = sin_tilt * sin_tilt
            coef[5, z] = 0.5 * sin_tilt * cos_tilt
            return carry

        lax.fori_loop(0, planes, plane, 0)

    def snap_copy(s, n):
        dx, other = SNAP_WAYS[n]
        return remote(
            snap_send.at[s],
            snap_recv.at[s, n],
            snap_ssem.at[s, n],
            snap_rsem.at[s, n],
            device(dx, 0, other),
        )

    lane = lax.broadcasted_iota(jnp.int32, (nx, ny), 1)
    keep = (lane < ny // 2) == is_source

    def place(s, section, dx, whole):
        start = nx - dx * nx
        whole = whole.astype(jnp.float32)
        own, other = split(whole[0].reshape(nz, nx, ny), whole[1].reshape(nz, nx, ny))
        centre[s, section, :, start : start + nx, :] = own
        beside[s, section, :, start : start + nx, :] = jnp.where(keep[None], other, 0.0)

    def send_snapshot(s, ref):
        for half in range(2):
            rounded = ref[0, DEEP : DEEP + nz, half, block, :].astype(jnp.bfloat16)
            snap_send[s, half] = rounded.reshape(nz * nx, ny)
        for n, (dx, other) in enumerate(SNAP_WAYS):
            guarded(exists(dx, 0), snap_copy(s, n).start)
        place(s, gy, 0, snap_send[s])

    def take_snapshot(s):
        for n, (dx, other) in enumerate(SNAP_WAYS):

            def go():
                snap_copy(s, n).wait_recv()
                place(s, 1 - gy if other else gy, dx, snap_recv[s, n])

            guarded(exists(-dx, 0), go)

    def image(s):
        some = 4 if nlag % 4 == 0 else 1

        def product(lag):
            lx = lag_ref[0, lag]
            ly = lag_ref[1, lag]

            def shifted(h, sx, sy):
                c = centre[s, h, :, pl.ds(nx + sx, nx), :]
                b = beside[s, h, :, pl.ds(nx + sx, nx), :]
                edge = jnp.logical_or(lane < sy, lane >= ny + sy)
                mixed = jnp.where(edge[None], b, c)
                return pltpu.roll(mixed, lax.rem(ny - sy, ny), 2)

            term = shifted(0, -lx, -ly) * shifted(1, lx, ly)
            term = term.reshape(nz * nx, ny)
            return term if s == 0 else acc[lag] + term

        def lags(i, carry):
            terms = [product(i * some + more) for more in range(some)]
            for more, term in enumerate(terms):
                if s < SNAPS - 1:
                    acc[i * some + more] = term
                else:
                    img_ref[i * some + more] = term.astype(jnp.bfloat16)
            return carry

        lax.fori_loop(0, nlag // some, lags, 0)

    def advance(j, halo, active, here, there):
        skip = SIDE if halo == 0 else 0
        start, stop = TOP + skip, TOP + window - skip
        rows = slice(start, stop)
        inner = slice(skip, window - skip)
        step_lane = lax.broadcasted_iota(jnp.int32, (stop - start, ny), 1)
        first_lane = step_lane == 0
        last_lane = step_lane == ny - 1
        for z in range(DEEP - halo, DEEP + nz + halo):
            c = z - 1
            left, right = here[0, z, 0, rows, :], here[0, z, 1, rows, :]
            left_up, right_up = pltpu.roll(left, ny - 1, 1), pltpu.roll(right, ny - 1, 1)
            left_down, right_down = pltpu.roll(left, 1, 1), pltpu.roll(right, 1, 1)
            sides = (
                jnp.where(last_lane, right_up, left_up) + jnp.where(first_lane, 0.0, left_down),
                jnp.where(last_lane, 0.0, right_up) + jnp.where(first_lane, left_down, right_down),
            )
            for half in range(2):

                def diffs(f):
                    def at(dz, dx):
                        return here[f, z + dz, half, start + dx : stop + dx, :]

                    mid = at(0, 0)
                    twice = 2.0 * mid
                    zz = at(1, 0) + at(-1, 0) - twice
                    xx = at(0, 1) + at(0, -1) - twice
                    xz = at(1, 1) - at(1, -1) - at(-1, 1) + at(-1, -1)
                    return mid, twice, zz, xx, xz

                p, twice_p, pzz, pxx, pxz = diffs(0)
                q, twice_q, qzz, qxx, qxz = diffs(1)
                pyy = sides[half] - twice_p
                wz, wx, wm = (coef[i, c, half, inner, :] for i in (3, 4, 5))
                vert_p = wz * pzz + wx * pxx + wm * pxz
                horiz = pzz + pxx + pyy - vert_p
                vert_q = wz * qzz + wx * qxx + wm * qxz
                p_old, q_old = old[0, z, half, rows, :], old[1, z, half, rows, :]
                amount = dep[j, c, half, inner, :]
                cou = coef[0, c, half, inner, :]
                new_p = twice_p - p_old + cou * (coef[1, c, half, inner, :] * horiz + vert_q) + amount
                new_q = twice_q - q_old + cou * (coef[2, c, half, inner, :] * horiz + vert_q) + amount
                there[0, z, half, rows, :] = jnp.where(active, new_p, p)
                there[1, z, half, rows, :] = jnp.where(active, new_q, q)
                old[0, z, half, rows, :] = jnp.where(active, p, p_old)
                old[1, z, half, rows, :] = jnp.where(active, q, q_old)

    def window_steps(s, carry):
        @pl.when(s > 0)
        def _():
            send_fields(s)
            send_snapshot(s - 1, now)
            deposits(s)


        @pl.when(s == SNAPS - 1)
        def _():
            take_snapshot(0)
            image(0)

        take_fields(s)
        here, there = now, new
        for j in range(STEPS):
            advance(j, STEPS - 1 - j, j < cnt_ref[s], here, there)
            here, there = there, here
        if here is new:
            for f in range(2):
                now[f, DEEP : DEEP + nz, :, block, :] = new[f, DEEP : DEEP + nz, :, block, :]
        return carry

    deposits(0)
    take_coefficients()
    swap_source.wait_recv()
    for i, (ref, f) in enumerate(field_arrays):
        left, right = joined(loaded[gy, i], theirs[i])
        ref[f, DEEP : DEEP + nz, 0, block, :] = left
        ref[f, DEEP : DEEP + nz, 1, block, :] = right
    coefficients()
    lax.fori_loop(0, SNAPS, window_steps, 0)

    send_snapshot(SNAPS - 1, now)
    for i, (ref, f) in enumerate(field_arrays):
        own, other = split(
            ref[f, DEEP : DEEP + nz, 0, block, :], ref[f, DEEP : DEEP + nz, 1, block, :]
        )
        both[gy, i] = own
        give[i] = other
    back = remote(give, both.at[gy], pair_ssem.at[2], pair_rsem.at[2], to_pair)
    back.start()
    for s in range(1, SNAPS - 1):
        take_snapshot(s)
        image(s)
    take_snapshot(SNAPS - 1)
    image(SNAPS - 1)
    remote(give, both.at[1 - gy], pair_ssem.at[2], pair_rsem.at[2], to_pair).wait_recv()
    so_ref[...] = both[0]
    ro_ref[...] = both[1]

    back.wait_send()
    share(gy).wait_send()
    swap_source.wait_send()
    for n, (dx, dz) in enumerate(WAYS):

        def ended():
            coef_copy(n).wait_send()
            for section in range(2):
                first_copy(n, section).wait_send()
            for s in range(1, SNAPS):
                field_copy(s, n).wait_send()

        guarded(exists(dx, dz), ended)
    for n, (dx, _) in enumerate(SNAP_WAYS):

        def ended():
            for s in range(SNAPS):
                snap_copy(s, n).wait_send()

        guarded(exists(dx, 0), ended)


def local(
    sizes,
    source_fields,
    receiver_fields,
    courant,
    epsilon,
    delta_param,
    tilt_angle,
    source_pos,
    wavelet,
    receiver_pos,
    receiver_data,
    step_counts,
    offset_lags,
):
    nz, nx, ny = courant.shape
    nlag = offset_lags.shape[0]
    f32, bf16 = jnp.float32, jnp.bfloat16
    vmem = pl.BlockSpec(memory_space=pltpu.VMEM)
    hbm = pl.BlockSpec(memory_space=pltpu.HBM)
    window = nx + 2 * SIDE
    whole = (nz + 2 * DEEP, 2, window + 2 * TOP, ny)
    inner = (nz + 2 * (DEEP - 1), 2, window, ny)
    field_rows = [message_rows(dx, dz, FIELD_DEPTHS, nz, nx) for dx, dz in WAYS]
    coef_rows = [message_rows(dx, dz, COEF_DEPTHS, nz, nx) for dx, dz in WAYS]
    images, source_out, receiver_out = pl.pallas_call(
        functools.partial(kernel, sizes),
        out_shape=(
            jax.ShapeDtypeStruct((nlag, nz * nx, ny), bf16),
            jax.ShapeDtypeStruct(source_fields.shape, f32),
            jax.ShapeDtypeStruct(receiver_fields.shape, f32),
        ),
        in_specs=[hbm] * 12,
        out_specs=(vmem, vmem, vmem),
        scratch_shapes=[
            pltpu.VMEM((2, *whole), f32),
            pltpu.VMEM((2, *whole), f32),
            pltpu.VMEM((2, *whole), f32),
            pltpu.VMEM((4, *whole), f32),
            pltpu.VMEM((6, *inner), f32),
            pltpu.VMEM((STEPS, *inner), f32),
            pltpu.VMEM((2, 4, nz, nx, ny), f32),
            pltpu.VMEM((4, nz, nx, ny), f32),
            pltpu.VMEM((4, nz, nx, ny), f32),
            *[pltpu.VMEM((SNAPS, 2, count, ny), f32) for count in field_rows * 2],
            *[pltpu.VMEM((count, ny), f32) for count in coef_rows * 2],
            pltpu.VMEM((SNAPS, 2, nz * nx, ny), bf16),
            pltpu.VMEM((SNAPS, len(SNAP_WAYS), 2, nz * nx, ny), bf16),
            pltpu.VMEM((SNAPS, 2, nz, 3 * nx, ny), f32),
            pltpu.VMEM((SNAPS, 2, nz, 3 * nx, ny), f32),
            pltpu.VMEM((nlag, nz * nx, ny), f32),
            pltpu.VMEM((2, 4, nz, nx, ny), f32),
            pltpu.VMEM((4, nz, nx, ny), f32),
            pltpu.SemaphoreType.DMA((12,)),
            pltpu.SemaphoreType.DMA((3,)),
            pltpu.SemaphoreType.DMA((3,)),
            pltpu.SemaphoreType.DMA((SNAPS + 1, len(WAYS))),
            pltpu.SemaphoreType.DMA((SNAPS + 1, len(WAYS))),
            pltpu.SemaphoreType.DMA((SNAPS, len(SNAP_WAYS))),
            pltpu.SemaphoreType.DMA((SNAPS, len(SNAP_WAYS))),
            pltpu.SemaphoreType.DMA((len(WAYS), 2)),
            pltpu.SemaphoreType.DMA((len(WAYS), 2)),
            *[pltpu.VMEM((2, count, ny), f32) for count in field_rows],
            pltpu.SMEM(source_pos.shape, jnp.int32),
            pltpu.SMEM(wavelet.shape, f32),
            pltpu.SMEM(step_counts.shape, jnp.int32),
            pltpu.SMEM(offset_lags.shape[::-1], jnp.int32),
            pltpu.VMEM(receiver_pos.shape[::-1], jnp.int32),
            pltpu.VMEM(receiver_data.shape, f32),
        ],
        compiler_params=pltpu.CompilerParams(
            collective_id=0, has_side_effects=True, vmem_limit_bytes=48 * 1024 * 1024
        ),
    )(
        *(
            pltpu.with_memory_space_constraint(x, pltpu.HBM)
            for x in (
                source_fields,
                receiver_fields,
                courant,
                epsilon,
                delta_param,
                tilt_angle,
                source_pos,
                wavelet,
                receiver_pos.T,
                receiver_data,
                step_counts,
                offset_lags.T,
            )
        )
    )
    return images.reshape(nlag, nz, nx, ny), source_out, receiver_out


def solution(mesh):
    fields = P("shot", "sec", "gx", "gy")
    grid = P("sec", "gx", "gy")
    sizes = tuple(mesh.shape[axis] for axis in ("gx", "sec", "gy"))
    return jax.shard_map(
        functools.partial(local, sizes),
        mesh=mesh,
        in_specs=(
            fields,
            fields,
            grid,
            grid,
            grid,
            grid,
            P("shot"),
            P("shot"),
            P("shot", None),
            P("shot", None),
            P(),
            P(),
        ),
        out_specs=(fields, fields, fields),
        check_vma=False,
    )
```

```python
import functools

import jax
import jax.numpy as jnp
from jax import lax
from jax.experimental import pallas as pl
from jax.experimental.pallas import tpu as pltpu
from jax.sharding import PartitionSpec as P

SNAPS = 3
STEPS = 3
DEEP = STEPS
MESH = pl.DeviceIdType.MESH

TOP = 8
SIDE = 4
WAYS = ((-1, -1), (-1, 1), (1, -1), (1, 1), (-1, 0), (1, 0), (0, -1), (0, 1))
SNAP_WAYS = ((-1, True), (1, True), (-1, False), (1, False), (0, True))


def layers(dx, dz, depth, nz, nx):
    if dz == 0:
        z_from, z_to, z_count = DEEP, DEEP, nz
    elif dz < 0:
        z_from, z_to, z_count = DEEP, DEEP + nz, depth
    else:
        z_from, z_to, z_count = DEEP + nz - depth, DEEP - depth, depth
    first = TOP + SIDE
    if dx == 0:
        x_from, x_to, x_count = first, first, nx
    elif dx < 0:
        x_from, x_to, x_count = first, first + nx, depth
    else:
        x_from, x_to, x_count = first + nx - depth, first - depth, depth
    return z_from, z_to, z_count, x_from, x_to, x_count


def message_rows(dx, dz, depths, nz, nx):
    total = 0
    for depth in depths:
        _, _, z_count, _, _, x_count = layers(dx, dz, depth, nz, nx)
        total += z_count * x_count
    return -(-total // 8) * 8


FIELD_DEPTHS = (DEEP, DEEP, DEEP - 1, DEEP - 1)
COEF_DEPTHS = (DEEP - 1,) * 4


def kernel(
    sizes,
    src_ref,
    rec_ref,
    cou_ref,
    eps_ref,
    del_ref,
    tilt_ref,
    spos_ref,
    wav_ref,
    rpos_ref,
    rdat_ref,
    cnt_ref,
    lag_ref,
    img_ref,
    so_ref,
    ro_ref,
    *scratch,
):
    small_hbm = (spos_ref, wav_ref, cnt_ref, lag_ref, rpos_ref, rdat_ref)
    small = scratch[-6:]
    spos_ref, wav_ref, cnt_ref, lag_ref, rpos_ref, rdat_ref = small
    scratch = scratch[:-6]
    now, new, old, raw, coef, dep = scratch[:6]
    loaded, theirs, coef_own = scratch[6:9]
    field_send, field_recv = scratch[9:17], scratch[17:25]
    coef_send, coef_recv = scratch[25:33], scratch[33:41]
    snap_send, snap_recv, centre, beside, acc, both, give = scratch[41:48]
    load_sem, pair_ssem, pair_rsem, halo_ssem, halo_rsem, snap_ssem, snap_rsem = scratch[48:55]
    first_ssem, first_rsem, *first_send = scratch[55:]
    nz, nx, ny = cou_ref.shape
    nlag = lag_ref.shape[1]
    window = nx + 2 * SIDE
    first = TOP + SIDE
    rows = slice(TOP, TOP + window)
    block = slice(first, first + nx)
    ngx, nsec, _ = sizes
    gx, sec, gy = lax.axis_index("gx"), lax.axis_index("sec"), lax.axis_index("gy")
    is_source = gy == 0

    def exists(dx, dz):
        ok = None
        if dx:
            ok = gx > 0 if dx < 0 else gx < ngx - 1
        if dz:
            okz = sec > 0 if dz < 0 else sec < nsec - 1
            ok = okz if ok is None else jnp.logical_and(ok, okz)
        return ok

    def guarded(ok, action):
        if ok is None:
            action()
        else:
            pl.when(ok)(action)

    def device(dx, dz, other):
        where = {}
        if dx:
            where["gx"] = gx + dx
        if dz:
            where["sec"] = sec + dz
        if other:
            where["gy"] = 1 - gy
        return where

    def remote(src, dst, send_sem, recv_sem, where):
        return pltpu.make_async_remote_copy(
            src_ref=src,
            dst_ref=dst,
            send_sem=send_sem,
            recv_sem=recv_sem,
            device_id=where,
            device_id_type=MESH,
        )

    coef_refs = (cou_ref, eps_ref, del_ref, tilt_ref)
    loads = [
        pltpu.make_async_copy(ref, coef_own.at[i], load_sem.at[i])
        for i, ref in enumerate(coef_refs)
    ]
    loads += [
        pltpu.make_async_copy(ref, held, load_sem.at[5 + i])
        for i, (ref, held) in enumerate(zip(small_hbm, small))
    ]
    loads += [
        pltpu.make_async_copy(src_ref, loaded.at[0], load_sem.at[4]),
        pltpu.make_async_copy(rec_ref, loaded.at[1], load_sem.at[11]),
    ]
    for copy in loads:
        copy.start()

    barrier = pltpu.get_barrier_semaphore()
    total = jnp.int32(1)
    to_pair = device(0, 0, True)
    pl.semaphore_signal(barrier, inc=1, device_id=to_pair, device_id_type=MESH)
    for dx, dz in WAYS:
        ok = exists(dx, dz)
        total = total + 2 * ok.astype(jnp.int32)

        @pl.when(ok)
        def _():
            for other in (False, True):
                pl.semaphore_signal(
                    barrier, inc=1, device_id=device(dx, dz, other), device_id_type=MESH
                )

    for ref in (now, old):
        ref[:, :, :, rows, :] = jnp.zeros(ref.shape[:3] + (window, ny), jnp.float32)
    raw[:, :, gy, rows, :] = jnp.zeros(raw.shape[:2] + (window, ny), jnp.float32)
    centre[...] = jnp.zeros_like(centre)
    beside[...] = jnp.zeros_like(beside)
    pl.semaphore_wait(barrier, total)

    swap_receiver = remote(rec_ref, theirs, pair_ssem.at[0], pair_rsem.at[0], to_pair)
    swap_source = remote(src_ref, theirs, pair_ssem.at[0], pair_rsem.at[0], to_pair)
    pl.when(is_source)(swap_receiver.start)
    pl.when(jnp.logical_not(is_source))(swap_source.start)

    def joined(own, other):
        left = jnp.where(is_source, own, other)
        right = jnp.where(is_source, other, own)
        return left, right

    def split(left, right):
        return jnp.where(is_source, left, right), jnp.where(is_source, right, left)

    def pack(buffer, arrays, depths, dx, dz):
        at = 0
        for (ref, f), depth in zip(arrays, depths):
            z_from, _, z_count, x_from, _, x_count = layers(dx, dz, depth, nz, nx)
            chunks = [
                ref[f, z_from + z, :, x_from : x_from + x_count, :] for z in range(z_count)
            ]
            for chunk in chunks:
                buffer[:, at : at + x_count, :] = chunk
                at += x_count

    def unpack(buffer, arrays, depths, dx, dz):
        at = 0
        for (ref, f), depth in zip(arrays, depths):
            _, z_to, z_count, _, x_to, x_count = layers(dx, dz, depth, nz, nx)
            chunks = []
            for z in range(z_count):
                chunks.append(buffer[:, at : at + x_count, :])
                at += x_count
            for z, chunk in enumerate(chunks):
                ref[f, z_to + z, :, x_to : x_to + x_count, :] = chunk

    field_arrays = [(now, 0), (now, 1), (old, 0), (old, 1)]

    def pack_block(buffer, blocks, depths, dx, dz):
        at = 0
        for block_ref, depth in zip(blocks, depths):
            z_from, _, z_count, x_from, _, x_count = layers(dx, dz, depth, nz, nx)
            z_from, x_from = z_from - DEEP, x_from - first
            chunks = [block_ref[z_from + z, x_from : x_from + x_count, :] for z in range(z_count)]
            for chunk in chunks:
                buffer[at : at + x_count, :] = chunk
                at += x_count

    def coef_copy(n):
        return remote(
            coef_send[n],
            coef_recv[n],
            halo_ssem.at[SNAPS, n],
            halo_rsem.at[SNAPS, n],
            device(*WAYS[n], False),
        )

    def first_copy(n, section):
        where = device(*WAYS[n], False)
        where["gy"] = section
        return remote(
            first_send[n].at[section],
            field_recv[n].at[0, gy],
            first_ssem.at[n, section],
            first_rsem.at[n, gy],
            where,
        )

    def field_copy(s, n):
        return remote(
            field_send[n].at[s],
            field_recv[n].at[s],
            halo_ssem.at[s, n],
            halo_rsem.at[s, n],
            device(*WAYS[n], False),
        )

    def send_fields(s):
        for n, (dx, dz) in enumerate(WAYS):

            def go():
                pack(field_send[n].at[s], field_arrays, FIELD_DEPTHS, dx, dz)
                field_copy(s, n).start()

            guarded(exists(dx, dz), go)

    def take_fields(s):
        for n, (dx, dz) in enumerate(WAYS):

            def go():
                @pl.when(s == 0)
                def _():
                    for half in range(2):
                        remote(
                            first_send[n].at[half],
                            field_recv[n].at[0, half],
                            first_ssem.at[n, half],
                            first_rsem.at[n, half],
                            to_pair,
                        ).wait_recv()

                pl.when(s > 0)(field_copy(s, n).wait_recv)
                unpack(field_recv[n].at[s], field_arrays, FIELD_DEPTHS, dx, dz)

            guarded(exists(-dx, -dz), go)

    for copy in loads:
        copy.wait()
    for n, (dx, dz) in enumerate(WAYS):

        def go():
            pack_block(
                coef_send[n], [coef_own.at[i] for i in range(4)], COEF_DEPTHS, dx, dz
            )
            coef_copy(n).start()

        guarded(exists(dx, dz), go)
    for n, (dx, dz) in enumerate(WAYS):

        def go():
            for section in range(2):
                blocks = [loaded.at[section, f] for f in range(4)]
                pack_block(first_send[n].at[section], blocks, FIELD_DEPTHS, dx, dz)
                first_copy(n, section).start()

        guarded(exists(dx, dz), go)
    for i in range(4):
        raw[i, DEEP : DEEP + nz, gy, block, :] = coef_own[i]

    planes = nz + 2 * (DEEP - 1)

    def deposits(s):
        nrec = rpos_ref.shape[1]
        lane = lax.broadcasted_iota(jnp.int32, (1, nrec), 1)

        def points(d):
            alone = jnp.where(lane == 0, spos_ref[d], -1)
            return jnp.where(is_source, alone, rpos_ref[d : d + 1, :])

        pz = points(0) - sec * nz + (DEEP - 1)
        px = points(1) - gx * nx + SIDE
        py = points(2)
        at_y = lax.broadcasted_iota(jnp.int32, (2 * ny, nrec), 0) == py
        at_y = jnp.where(at_y, 1.0, 0.0).astype(jnp.bfloat16)
        cell = jnp.where((px >= 0) & (px < window), pz * window + px, -1)
        at_cell = lax.broadcasted_iota(jnp.int32, (planes * window, nrec), 0) == cell
        for j in range(STEPS):
            t = s * STEPS + j
            alone = jnp.where(lane == 0, wav_ref[t], 0.0)
            amounts = jnp.where(is_source, alone, rdat_ref[pl.ds(t, 1), :])
            high = amounts.astype(jnp.bfloat16).astype(jnp.float32)
            summed = None
            for part in (high, amounts - high):
                picked = jnp.where(at_cell, part, 0.0).astype(jnp.bfloat16)
                term = lax.dot_general(
                    picked, at_y, (((1,), (1,)), ((), ())), preferred_element_type=jnp.float32
                )
                summed = term if summed is None else summed + term
            for half in range(2):
                lanes = summed[:, half * ny : (half + 1) * ny]
                dep[j, :, half] = lanes.reshape(planes, window, ny)

    def share(half):
        part = raw.at[:, 1 : 1 + planes, half, rows, :]
        return remote(part, part, pair_ssem.at[1], pair_rsem.at[1], to_pair)

    def take_coefficients():
        for n, (dx, dz) in enumerate(WAYS):

            def go():
                coef_copy(n).wait_recv()
                at = 0
                for i, depth in enumerate(COEF_DEPTHS):
                    _, z_to, z_count, _, x_to, x_count = layers(dx, dz, depth, nz, nx)
                    chunks = []
                    for z in range(z_count):
                        chunks.append(coef_recv[n][at : at + x_count, :])
                        at += x_count
                    for z, chunk in enumerate(chunks):
                        raw[i, z_to + z, gy, x_to : x_to + x_count, :] = chunk

            guarded(exists(-dx, -dz), go)
        share(gy).start()

    def coefficients():
        share(1 - gy).wait_recv()

        def plane(z, carry):
            tilt = raw[3, 1 + z, :, rows, :]
            cos_tilt, sin_tilt = jnp.cos(tilt), jnp.sin(tilt)
            coef[0, z] = raw[0, 1 + z, :, rows, :]
            coef[1, z] = 1.0 + 2.0 * raw[1, 1 + z, :, rows, :]
            coef[2, z] = 1.0 + 2.0 * raw[2, 1 + z, :, rows, :]
            coef[3, z] = cos_tilt * cos_tilt
            coef[4, z] = sin_tilt * sin_tilt
            coef[5, z] = 0.5 * sin_tilt * cos_tilt
            return carry

        lax.fori_loop(0, planes, plane, 0)

    def snap_copy(s, n):
        dx, other = SNAP_WAYS[n]
        return remote(
            snap_send.at[s],
            snap_recv.at[s, n],
            snap_ssem.at[s, n],
            snap_rsem.at[s, n],
            device(dx, 0, other),
        )

    lane = lax.broadcasted_iota(jnp.int32, (nx, ny), 1)
    keep = (lane < ny // 2) == is_source

    def place(s, section, dx, whole):
        start = nx - dx * nx
        whole = whole.astype(jnp.float32)
        own, other = split(whole[0].reshape(nz, nx, ny), whole[1].reshape(nz, nx, ny))
        centre[s, section, :, start : start + nx, :] = own
        beside[s, section, :, start : start + nx, :] = jnp.where(keep[None], other, 0.0)

    def send_snapshot(s, ref):
        for half in range(2):
            rounded = ref[0, DEEP : DEEP + nz, half, block, :].astype(jnp.bfloat16)
            snap_send[s, half] = rounded.reshape(nz * nx, ny)
        for n, (dx, other) in enumerate(SNAP_WAYS):
            guarded(exists(dx, 0), snap_copy(s, n).start)
        place(s, gy, 0, snap_send[s])

    def take_snapshot(s):
        for n, (dx, other) in enumerate(SNAP_WAYS):

            def go():
                snap_copy(s, n).wait_recv()
                place(s, 1 - gy if other else gy, dx, snap_recv[s, n])

            guarded(exists(-dx, 0), go)

    def image(s):
        some = 4 if nlag % 4 == 0 else 1

        def product(lag):
            lx = lag_ref[0, lag]
            ly = lag_ref[1, lag]

            def shifted(h, sx, sy):
                c = centre[s, h, :, pl.ds(nx + sx, nx), :]
                b = beside[s, h, :, pl.ds(nx + sx, nx), :]
                edge = jnp.logical_or(lane < sy, lane >= ny + sy)
                mixed = jnp.where(edge[None], b, c)
                return pltpu.roll(mixed, lax.rem(ny - sy, ny), 2)

            term = shifted(0, -lx, -ly) * shifted(1, lx, ly)
            term = term.reshape(nz * nx, ny)
            return term if s == 0 else acc[lag] + term

        def lags(i, carry):
            terms = [product(i * some + more) for more in range(some)]
            for more, term in enumerate(terms):
                if s < SNAPS - 1:
                    acc[i * some + more] = term
                else:
                    img_ref[i * some + more] = term.astype(jnp.bfloat16)
            return carry

        lax.fori_loop(0, nlag // some, lags, 0)

    def advance(j, halo, active, here, there):
        skip = SIDE if halo == 0 else 0
        start, stop = TOP + skip, TOP + window - skip
        rows = slice(start, stop)
        inner = slice(skip, window - skip)
        step_lane = lax.broadcasted_iota(jnp.int32, (stop - start, ny), 1)
        first_lane = step_lane == 0
        last_lane = step_lane == ny - 1
        for z in range(DEEP - halo, DEEP + nz + halo):
            c = z - 1
            left, right = here[0, z, 0, rows, :], here[0, z, 1, rows, :]
            left_up, right_up = pltpu.roll(left, ny - 1, 1), pltpu.roll(right, ny - 1, 1)
            left_down, right_down = pltpu.roll(left, 1, 1), pltpu.roll(right, 1, 1)
            sides = (
                jnp.where(last_lane, right_up, left_up) + jnp.where(first_lane, 0.0, left_down),
                jnp.where(last_lane, 0.0, right_up) + jnp.where(first_lane, left_down, right_down),
            )
            for half in range(2):

                def diffs(f):
                    def at(dz, dx):
                        return here[f, z + dz, half, start + dx : stop + dx, :]

                    mid = at(0, 0)
                    twice = 2.0 * mid
                    zz = at(1, 0) + at(-1, 0) - twice
                    xx = at(0, 1) + at(0, -1) - twice
                    xz = at(1, 1) - at(1, -1) - at(-1, 1) + at(-1, -1)
                    return mid, twice, zz, xx, xz

                p, twice_p, pzz, pxx, pxz = diffs(0)
                q, twice_q, qzz, qxx, qxz = diffs(1)
                pyy = sides[half] - twice_p
                wz, wx, wm = (coef[i, c, half, inner, :] for i in (3, 4, 5))
                vert_p = wz * pzz + wx * pxx + wm * pxz
                horiz = pzz + pxx + pyy - vert_p
                vert_q = wz * qzz + wx * qxx + wm * qxz
                p_old, q_old = old[0, z, half, rows, :], old[1, z, half, rows, :]
                amount = dep[j, c, half, inner, :]
                cou = coef[0, c, half, inner, :]
                new_p = twice_p - p_old + cou * (coef[1, c, half, inner, :] * horiz + vert_q) + amount
                new_q = twice_q - q_old + cou * (coef[2, c, half, inner, :] * horiz + vert_q) + amount
                there[0, z, half, rows, :] = jnp.where(active, new_p, p)
                there[1, z, half, rows, :] = jnp.where(active, new_q, q)
                old[0, z, half, rows, :] = jnp.where(active, p, p_old)
                old[1, z, half, rows, :] = jnp.where(active, q, q_old)

    def window_steps(s, carry):
        @pl.when(s > 0)
        def _():
            send_fields(s)
            send_snapshot(s - 1, now)
            deposits(s)


        @pl.when(s == SNAPS - 1)
        def _():
            take_snapshot(0)
            image(0)

        take_fields(s)
        here, there = now, new
        for j in range(STEPS):
            advance(j, STEPS - 1 - j, j < cnt_ref[s], here, there)
            here, there = there, here
        if here is new:
            for f in range(2):
                now[f, DEEP : DEEP + nz, :, block, :] = new[f, DEEP : DEEP + nz, :, block, :]
        return carry

    deposits(0)
    take_coefficients()
    swap_source.wait_recv()
    for i, (ref, f) in enumerate(field_arrays):
        left, right = joined(loaded[gy, i], theirs[i])
        ref[f, DEEP : DEEP + nz, 0, block, :] = left
        ref[f, DEEP : DEEP + nz, 1, block, :] = right
    coefficients()
    lax.fori_loop(0, SNAPS, window_steps, 0)

    send_snapshot(SNAPS - 1, now)
    for i, (ref, f) in enumerate(field_arrays):
        own, other = split(
            ref[f, DEEP : DEEP + nz, 0, block, :], ref[f, DEEP : DEEP + nz, 1, block, :]
        )
        both[gy, i] = own
        give[i] = other
    back = remote(give, both.at[gy], pair_ssem.at[2], pair_rsem.at[2], to_pair)
    back.start()
    for s in range(1, SNAPS - 1):
        take_snapshot(s)
        image(s)
    take_snapshot(SNAPS - 1)
    image(SNAPS - 1)
    remote(give, both.at[1 - gy], pair_ssem.at[2], pair_rsem.at[2], to_pair).wait_recv()
    so_ref[...] = both[0]
    ro_ref[...] = both[1]

    back.wait_send()
    share(gy).wait_send()
    swap_source.wait_send()
    for n, (dx, dz) in enumerate(WAYS):

        def ended():
            coef_copy(n).wait_send()
            for section in range(2):
                first_copy(n, section).wait_send()
            for s in range(1, SNAPS):
                field_copy(s, n).wait_send()

        guarded(exists(dx, dz), ended)
    for n, (dx, _) in enumerate(SNAP_WAYS):

        def ended():
            for s in range(SNAPS):
                snap_copy(s, n).wait_send()

        guarded(exists(dx, 0), ended)


def local(
    sizes,
    source_fields,
    receiver_fields,
    courant,
    epsilon,
    delta_param,
    tilt_angle,
    source_pos,
    wavelet,
    receiver_pos,
    receiver_data,
    step_counts,
    offset_lags,
):
    nz, nx, ny = courant.shape
    nlag = offset_lags.shape[0]
    f32, bf16 = jnp.float32, jnp.bfloat16
    vmem = pl.BlockSpec(memory_space=pltpu.VMEM)
    hbm = pl.BlockSpec(memory_space=pltpu.HBM)
    window = nx + 2 * SIDE
    whole = (nz + 2 * DEEP, 2, window + 2 * TOP, ny)
    inner = (nz + 2 * (DEEP - 1), 2, window, ny)
    field_rows = [message_rows(dx, dz, FIELD_DEPTHS, nz, nx) for dx, dz in WAYS]
    coef_rows = [message_rows(dx, dz, COEF_DEPTHS, nz, nx) for dx, dz in WAYS]
    images, source_out, receiver_out = pl.pallas_call(
        functools.partial(kernel, sizes),
        out_shape=(
            jax.ShapeDtypeStruct((nlag, nz * nx, ny), bf16),
            jax.ShapeDtypeStruct(source_fields.shape, f32),
            jax.ShapeDtypeStruct(receiver_fields.shape, f32),
        ),
        in_specs=[hbm] * 12,
        out_specs=(vmem, vmem, vmem),
        scratch_shapes=[
            pltpu.VMEM((2, *whole), f32),
            pltpu.VMEM((2, *whole), f32),
            pltpu.VMEM((2, *whole), f32),
            pltpu.VMEM((4, *whole), f32),
            pltpu.VMEM((6, *inner), f32),
            pltpu.VMEM((STEPS, *inner), f32),
            pltpu.VMEM((2, 4, nz, nx, ny), f32),
            pltpu.VMEM((4, nz, nx, ny), f32),
            pltpu.VMEM((4, nz, nx, ny), f32),
            *[pltpu.VMEM((SNAPS, 2, count, ny), f32) for count in field_rows * 2],
            *[pltpu.VMEM((count, ny), f32) for count in coef_rows * 2],
            pltpu.VMEM((SNAPS, 2, nz * nx, ny), bf16),
            pltpu.VMEM((SNAPS, len(SNAP_WAYS), 2, nz * nx, ny), bf16),
            pltpu.VMEM((SNAPS, 2, nz, 3 * nx, ny), f32),
            pltpu.VMEM((SNAPS, 2, nz, 3 * nx, ny), f32),
            pltpu.VMEM((nlag, nz * nx, ny), f32),
            pltpu.VMEM((2, 4, nz, nx, ny), f32),
            pltpu.VMEM((4, nz, nx, ny), f32),
            pltpu.SemaphoreType.DMA((12,)),
            pltpu.SemaphoreType.DMA((3,)),
            pltpu.SemaphoreType.DMA((3,)),
            pltpu.SemaphoreType.DMA((SNAPS + 1, len(WAYS))),
            pltpu.SemaphoreType.DMA((SNAPS + 1, len(WAYS))),
            pltpu.SemaphoreType.DMA((SNAPS, len(SNAP_WAYS))),
            pltpu.SemaphoreType.DMA((SNAPS, len(SNAP_WAYS))),
            pltpu.SemaphoreType.DMA((len(WAYS), 2)),
            pltpu.SemaphoreType.DMA((len(WAYS), 2)),
            *[pltpu.VMEM((2, count, ny), f32) for count in field_rows],
            pltpu.SMEM(source_pos.shape, jnp.int32),
            pltpu.SMEM(wavelet.shape, f32),
            pltpu.SMEM(step_counts.shape, jnp.int32),
            pltpu.SMEM(offset_lags.shape[::-1], jnp.int32),
            pltpu.VMEM(receiver_pos.shape[::-1], jnp.int32),
            pltpu.VMEM(receiver_data.shape, f32),
        ],
        compiler_params=pltpu.CompilerParams(
            collective_id=0, has_side_effects=True, vmem_limit_bytes=48 * 1024 * 1024
        ),
    )(
        *(
            pltpu.with_memory_space_constraint(x, pltpu.HBM)
            for x in (
                source_fields,
                receiver_fields,
                courant,
                epsilon,
                delta_param,
                tilt_angle,
                source_pos,
                wavelet,
                receiver_pos.T,
                receiver_data,
                step_counts,
                offset_lags.T,
            )
        )
    )
    return images.reshape(nlag, nz, nx, ny), source_out, receiver_out


def solution(mesh):
    fields = P("shot", "sec", "gx", "gy")
    grid = P("sec", "gx", "gy")
    sizes = tuple(mesh.shape[axis] for axis in ("gx", "sec", "gy"))
    return jax.shard_map(
        functools.partial(local, sizes),
        mesh=mesh,
        in_specs=(
            fields,
            fields,
            grid,
            grid,
            grid,
            grid,
            P("shot"),
            P("shot"),
            P("shot", None),
            P("shot", None),
            P(),
            P(),
        ),
        out_specs=(fields, fields, fields),
        check_vma=False,
    )
```
